128 devices in a mesh: pb: 8 (over z, x_lo), dev: 16 (over y, x_hi, core).
Axes of the slice: x: 4 (x_hi: 2, x_lo: 2; x = x_hi * 2 + x_lo), y: 4, z: 4, core: 2. Of those that a mesh axis runs over, the one named last changes fastest.
Arguments:
- q_hidden: bfloat16 [16384, 1024], P(('pb', 'dev')), may hold values from -60 to 60
- d_hidden: bfloat16 [16384, 1024], P(('dev', 'pb')), may hold values from -60 to 60
- positive: int32 [16384], P(('pb', 'dev')), may hold values from 0 to 16383, each once
- query_part: int32 [16384], P(('pb', 'dev')), may hold values from 0 to 7
- doc_part: int32 [16384], P(('dev', 'pb')), may hold values from 0 to 7
- loss_weight: bfloat16 [16384], P(('pb', 'dev')), may hold values from 0.5 to 5
- norm_gain: float32 [1024], replicated, may hold values from 0.5 to 1.5
- norm_bias: float32 [1024], replicated, may hold values from -1.8 to 1.8
- proj: bfloat16 [1024, 1024], replicated, may hold values from -0.1875 to 0.1875
Outputs:
- dq_hidden: bfloat16 [16384, 1024], P(('pb', 'dev'))
- dd_hidden: bfloat16 [16384, 1024], P(('dev', 'pb'))
- d_proj: float32 [1024, 1024], P('pb', 'dev')
- d_gain: float32 [1024], replicated
- d_bias: float32 [1024], replicated
The draws below stay inside these ranges and needn't reach their ends.
Inputs may be any that keep to these rules, and one draw needn't show every extreme that they name: `positive`: each document index names the clicked document of exactly one query.
All inputs are finite; a program needn't handle non-finite values.
Results may differ from the reference program's by a relative error of at most 0.024.
Values may be sent and summed in bfloat16 or wider, within the bound.
A program may use at most 128 MiB of HBM per device.

```python
import math
import jax
import jax.numpy as jnp
from jax import lax

D = 1024
E = 1024
NPART = 8
B = 16384


def paired_hidden(key, mixing):
    keys = jax.random.split(key, 6)
    base_q = jnp.clip(jax.random.normal(keys[0], (B, D), jnp.float32), -6.0, 6.0)
    base_d = jnp.clip(jax.random.normal(keys[1], (B, D), jnp.float32), -6.0, 6.0)
    index = jnp.arange(B)
    share = mixing * (index < 16).astype(jnp.float32)[:, None]
    docs = (1.0 - share) * base_d
    scale_q = jnp.exp(jax.random.uniform(keys[4], (B, 1), jnp.float32, 0.0, math.log(10.0)))
    scale_d = jnp.exp(jax.random.uniform(keys[5], (B, 1), jnp.float32, 0.0, math.log(10.0)))
    return (base_q * scale_q, docs * scale_d)


def draw_q_hidden(key, part):
    both = paired_hidden(key, 0.0)
    return both[0].astype(jnp.bfloat16)


def draw_d_hidden(key, part):
    both = paired_hidden(key, 0.0)
    return both[1].astype(jnp.bfloat16)


def touch_ends(result, key, smallest, largest):
    place = [jax.random.randint(jax.random.fold_in(key, axis), (), 0, length) for axis, length in enumerate(result.shape)]
    widest = result.shape.index(max(result.shape))
    beside = place[:widest] + [(place[widest] + 1) % result.shape[widest]] + place[widest + 1:]
    return result.at[tuple(place)].set(smallest).at[tuple(beside)].set(largest)


def shard_levels(key, dims, cuts, low, largest):
    gain, own = 1.0, jax.random.fold_in(key, 6)
    for position, shards_of in cuts:
        draws = jnp.exp(jax.random.uniform(jax.random.fold_in(own, position), (shards_of,), jnp.float32, low / len(cuts), largest / len(cuts)))
        gain = gain * jnp.repeat(draws, dims[position] // shards_of).reshape([-1 if axis == position else 1 for axis in range(len(dims))])
    return gain


def scatter_about(rng, extent, scale, most, kind=jnp.bfloat16):
    array = scale * jax.random.normal(rng, extent, jnp.float32)
    return jnp.clip(array, min=-most, max=most).astype(kind)


def setup_inputs(seed: int = 0) -> dict:
    key_of = jax.random.split(jax.random.key(seed), 10)
    return {
        "q_hidden": draw_q_hidden(jax.random.fold_in(key_of[9], 71), 0),
        "d_hidden": draw_d_hidden(jax.random.fold_in(key_of[9], 71), 0),
        "positive": jax.random.permutation(key_of[2], B).astype(jnp.int32),
        "query_part": touch_ends(jax.random.randint(key_of[3], (B,), 0, NPART), jax.random.fold_in(key_of[3], 1), 0, NPART - 1).astype(jnp.int32),
        "doc_part": touch_ends(jax.random.randint(key_of[4], (B,), 0, NPART), jax.random.fold_in(key_of[4], 1), 0, NPART - 1).astype(jnp.int32),
        "loss_weight": jnp.clip(jnp.exp(math.log(5.0) - 2.3025851 * jax.random.uniform(key_of[5], (B,), jnp.float32) ** shard_levels(key_of[5], (B,), ((0, 128),), -0.2, 0.2)), 0.5, 5.0).astype(jnp.bfloat16),
        "norm_gain": jnp.clip(1.0 + 0.1 * jax.random.normal(key_of[6], (D,), jnp.float32), 0.5, 1.5),
        "norm_bias": scatter_about(key_of[7], (D,), 0.3, 1.8, jnp.float32),
        "proj": scatter_about(key_of[8], (D, E), D ** -0.5, 0.1875),
    }


logit_scale = 100.0

def forward_rows(hidden, norm_gain, norm_bias, proj):
    values = hidden.astype(jnp.float32)
    centred = values - lax.optimization_barrier(jnp.mean(values, axis=1, keepdims=True))
    recip = lax.rsqrt(lax.optimization_barrier(jnp.mean(centred * centred, axis=1, keepdims=True)) + 1e-05)
    normed = centred * recip
    normal_out = (normed * norm_gain + norm_bias).astype(jnp.bfloat16)
    embed = jnp.dot(normal_out, proj, preferred_element_type=jnp.float32)
    inverse = lax.rsqrt(lax.optimization_barrier(jnp.sum(embed * embed, axis=1, keepdims=True)) + 1e-06)
    return (normed, recip, normal_out, embed * inverse, inverse)

def backward_rows(g_unit, normed, recip, unit, inverse, norm_gain, proj):
    g_embed = ((g_unit - unit * lax.optimization_barrier(jnp.sum(unit * g_unit, axis=1, keepdims=True))) * inverse).astype(jnp.bfloat16)
    g_normal = jnp.dot(g_embed, proj.T, preferred_element_type=jnp.float32)
    scaled = g_normal * norm_gain
    grad_h = recip * (scaled - lax.optimization_barrier(jnp.mean(scaled, axis=1, keepdims=True)) - normed * lax.optimization_barrier(jnp.mean(scaled * normed, axis=1, keepdims=True)))
    return (grad_h.astype(jnp.bfloat16), g_embed, g_normal)

def reference(q_hidden, d_hidden, positive, query_part, doc_part, loss_weight, norm_gain, norm_bias, proj):
    normed_q, recip_q, out_q, unit_q, inv_q = forward_rows(q_hidden, norm_gain, norm_bias, proj)
    normed_d, recip_d, out_d, unit_d, inv_d = forward_rows(d_hidden, norm_gain, norm_bias, proj)
    unit_qb = unit_q.astype(jnp.bfloat16)
    unit_db = unit_d.astype(jnp.bfloat16)
    block = math.gcd(B, 1024)
    count = B // block
    columns = jnp.arange(B, dtype=jnp.int32)

    def step(carry, index):
        start = (index * block).astype(jnp.int32)
        q_rows = lax.dynamic_slice_in_dim(unit_qb, start, block, 0)
        pos_rows = lax.dynamic_slice_in_dim(positive, start, block, 0)
        part_rows = lax.dynamic_slice_in_dim(query_part, start, block, 0)
        weight_rows = lax.dynamic_slice_in_dim(loss_weight, start, block, 0).astype(jnp.float32)
        scores = logit_scale * jnp.dot(q_rows, unit_db.T, preferred_element_type=jnp.float32)
        is_pos = pos_rows[:, None] == columns[None, :]
        valid = jnp.logical_or(part_rows[:, None] != doc_part[None, :], is_pos)
        masked = jnp.where(valid, scores, jnp.float32(-1e+30))
        top = lax.optimization_barrier(jnp.max(masked, axis=1, keepdims=True))
        total = lax.optimization_barrier(jnp.sum(jnp.where(valid, jnp.exp(masked - top), jnp.float32(0.0)), axis=1, keepdims=True))
        lse = top + jnp.log(total)
        prob = jnp.where(valid, jnp.exp(masked - lse), jnp.float32(0.0))
        grad = (weight_rows[:, None] * (prob - is_pos.astype(jnp.float32))).astype(jnp.bfloat16)
        g_query = logit_scale * jnp.dot(grad, unit_db, preferred_element_type=jnp.float32)
        carry = carry + logit_scale * jnp.dot(grad.T, q_rows, preferred_element_type=jnp.float32)
        return (carry, g_query)
    g_doc, g_query_blocks = lax.scan(step, jnp.zeros((B, E), jnp.float32), jnp.arange(count, dtype=jnp.int32))
    g_query = g_query_blocks.reshape(B, E)
    dq_hidden, ge_q, gn_q = backward_rows(g_query, normed_q, recip_q, unit_q, inv_q, norm_gain, proj)
    dd_hidden, ge_d, gn_d = backward_rows(g_doc, normed_d, recip_d, unit_d, inv_d, norm_gain, proj)
    d_proj = jnp.dot(out_q.T, ge_q, preferred_element_type=jnp.float32) + jnp.dot(out_d.T, ge_d, preferred_element_type=jnp.float32)
    d_gain = lax.optimization_barrier(jnp.sum(gn_q * normed_q, axis=0)) + lax.optimization_barrier(jnp.sum(gn_d * normed_d, axis=0))
    d_bias = lax.optimization_barrier(jnp.sum(gn_q, axis=0)) + lax.optimization_barrier(jnp.sum(gn_d, axis=0))
    return (dq_hidden, dd_hidden, d_proj, d_gain, d_bias)
```

```python
import jax
import jax.numpy as jnp
from jax import lax
from jax.experimental import pallas as pl
from jax.experimental.pallas import tpu as pltpu
from jax.sharding import PartitionSpec as P

logit_scale = 100.0
f32, bf16 = jnp.float32, jnp.bfloat16
MESH = pl.DeviceIdType.MESH
rows, width = 128, 1024
half = rows // 2
copies = 160
OFFSETS = ((0, 0), (0, 1), (0, 3), (1, 0), (1, 1), (1, 3), (0, 2), (1, 2))
NT = (((1,), (1,)), ((), ()))


def kernel(
    qh, dh, lab_q, lab_d, gain, bias, proj_hbm,
    dq, dd, dproj, dgb,
    proj, qbuf, dbuf, dt, st, gt, unit, normed, recip, inv, out_t, labs, dlab, dcol, mst, sst, lsend, lbuf,
    lsef, lrel, gqp, cbuf, sbuf, qfold, qring, qx, gdp, dfold, dring, dx_buf,
    ge, hp, hc, hs, hz1, hy1, h0, h1, hy2, hz2, hx, hx3, hf, hfs, gb, gba, gbb,
    send_sem, recv_sem, local_sem,
):
    pb, dev = lax.axis_index("pb"), lax.axis_index("dev")
    z, xl = pb // 2, lax.rem(pb, 2)
    y, xh, core = dev // 4, lax.rem(dev // 2, 2), lax.rem(dev, 2)

    def dev_at(dx, dy, dc):
        return lax.rem(y + dy, 4) * 4 + lax.rem(xh + dx, 2) * 2 + lax.rem(core + dc, 2)

    def pb_at(dx, dz):
        return lax.rem(z + dz, 4) * 2 + lax.rem(xl + dx, 2)

    def q_peer(dx, dy, dc=0):
        return (pb, dev_at(dx, dy, dc))

    def d_peer(dx, dz):
        return (pb_at(dx, dz), dev)

    started = []

    def send(src, dst, peer):
        n = len(started)
        copy = pltpu.make_async_remote_copy(
            src_ref=src, dst_ref=dst, send_sem=send_sem.at[n], recv_sem=recv_sem.at[n],
            device_id=peer, device_id_type=MESH,
        )
        copy.start()
        started.append(copy)
        return copy

    dev_offsets = [(dx, dy, dc) for dx in range(2) for dy in range(4) for dc in range(2)]
    pb_offsets = [(dx, dz) for dx in range(2) for dz in range(4)]

    load = pltpu.make_async_copy(proj_hbm, proj, local_sem)
    load.start()
    barrier = pltpu.get_barrier_semaphore()
    peers = [q_peer(*o) for o in dev_offsets[1:]] + [d_peer(*o) for o in pb_offsets[1:]]
    peers.append((pb_at(1, 0), dev_at(1, 0, 0)))
    for peer in peers:
        pl.semaphore_signal(barrier, inc=1, device_id=peer, device_id_type=MESH)

    values = jnp.concatenate([qh[...], dh[...]], axis=0).astype(f32)
    centred = values - jnp.mean(values, axis=1, keepdims=True)
    r = lax.rsqrt(jnp.mean(centred * centred, axis=1, keepdims=True) + 1e-05)
    norm = centred * r
    recip[...] = r
    normed[...] = norm
    normal_out = (norm * gain[...] + bias[...]).astype(bf16)
    load.wait()
    embed = jnp.dot(normal_out, proj[...], preferred_element_type=f32)
    i = lax.rsqrt(jnp.sum(embed * embed, axis=1, keepdims=True) + 1e-06)
    inv[...] = i
    u = embed * i
    unit[...] = u
    qbuf[0:rows, :] = u[:rows].astype(bf16)
    dbuf[0:rows, :] = u[rows:].astype(bf16)

    pl.semaphore_wait(barrier, len(peers))

    def q_slot(k, dc=0):
        return qbuf.at[pl.ds(k * 2 * rows + dc * rows, rows), :]

    def q_half(k, h):
        return qbuf.at[pl.ds(k * 2 * rows + h * half, half), :]

    def d_slot(k):
        return dbuf.at[pl.ds(k * rows, rows), :]

    def d_half(k, h):
        return dbuf.at[pl.ds(k * rows + h * half, half), :]

    def gather_own(slot, peer):
        return [send(slot(0), slot(3), peer(1, 0)), send(slot(0), slot(2), peer(0, 1)), send(slot(0), slot(1), peer(0, 3))]

    def gather_partner(slot, peer):
        return [send(slot(3), slot(5), peer(0, 1)), send(slot(3), slot(4), peer(0, 3))]

    def gather_far(part, peer, minus, plus, far):
        return [send(part(minus, 0), part(far, 0), peer(0, 1)), send(part(plus, 1), part(far, 1), peer(0, 3))]

    def to_sibling(k):
        return send(q_slot(k), q_slot(k, 1), q_peer(0, 0, 1))

    q_own = gather_own(q_slot, q_peer)
    d_own = gather_own(d_slot, d_peer)
    sib = {0: to_sibling(0)}
    lab_copies = []
    for s, (dx, dy, dc) in enumerate(dev_offsets):
        k = OFFSETS.index((dx, (4 - dy) % 4)) * 2 + dc
        dst = labs.at[:, pl.ds(k * rows, rows)]
        if s:
            lab_copies.append(send(lab_q, dst, q_peer(dx, dy, dc)))
    labs[:, 0:rows] = lab_q[...]
    for s, (dx, dz) in enumerate(pb_offsets):
        k = OFFSETS.index((dx, (4 - dz) % 4))
        if s:
            lab_copies.append(send(lab_d, dlab.at[k], d_peer(dx, dz)))
    dlab[0] = lab_d[...]

    out_t[...] = normal_out.T
    for copy in lab_copies:
        copy.wait_recv()
    for k in range(8):
        dcol[k * rows : (k + 1) * rows, :] = jnp.broadcast_to(dlab[k, 0:1, :], (rows, rows)).T

    def transpose_docs(first, count):
        for k in range(first, first + count):
            dt[:, k * rows : (k + 1) * rows] = dbuf[k * rows : (k + 1) * rows, :].T

    lane = lax.broadcasted_iota(jnp.int32, (rows, 2 * rows), 0).astype(f32)

    def bases(k):
        return (dev * (8 * rows) + pb_at(*OFFSETS[k]) * rows).astype(f32)

    def score(first, count, block, g):
        cols = pl.ds(pl.multiple_of(g * 2 * rows, 2 * rows), 2 * rows)
        s = logit_scale * lax.dot_general(
            dbuf[first * rows : (first + count) * rows, :], qbuf[cols, :], NT, preferred_element_type=f32
        )
        pos, part = labs[0:1, cols], labs[1:2, cols]
        masked = []
        for n in range(count):
            k = first + n
            col = dcol[k * rows : (k + 1) * rows, :]
            valid = jnp.logical_or(part != jnp.concatenate([col, col], axis=1), lane == pos - bases(k))
            masked.append(jnp.where(valid, s[n * rows : (n + 1) * rows], jnp.float32(-1e30)))
        top = jnp.full((1, 2 * rows), -1e4, f32)
        for m in masked:
            top = jnp.maximum(top, jnp.max(m, axis=0, keepdims=True))
        total = jnp.zeros((1, 2 * rows), f32)
        for n, m in enumerate(masked):
            p = jnp.exp(m - top)
            total = total + jnp.sum(p, axis=0, keepdims=True)
            st[(first + n) * rows : (first + n + 1) * rows, cols] = p
        mst[block, :, cols] = top
        sst[block, :, cols] = total

    def scores(first, count, block, low, high):
        lax.fori_loop(low, high, lambda g, c: (score(first, count, block, g), c)[1], 0)

    q_own[0].wait_recv()
    q_partner = gather_partner(q_slot, q_peer)
    sib[3] = to_sibling(3)
    d_own[0].wait_recv()
    d_partner = gather_partner(d_slot, d_peer)
    q_own[1].wait_recv()
    q_own[2].wait_recv()
    q_far = gather_far(q_half, q_peer, 2, 1, 6)
    sib[1], sib[2] = to_sibling(1), to_sibling(2)
    d_own[1].wait_recv()
    d_own[2].wait_recv()
    d_far = gather_far(d_half, d_peer, 2, 1, 6)
    transpose_docs(0, 4)
    for k in range(4):
        sib[k].wait_recv()
    scores(0, 4, 0, 0, 4)

    q_partner[0].wait_recv()
    q_partner[1].wait_recv()
    q_far += gather_far(q_half, q_peer, 5, 4, 7)
    sib[4], sib[5] = to_sibling(4), to_sibling(5)
    d_partner[0].wait_recv()
    d_partner[1].wait_recv()
    d_far += gather_far(d_half, d_peer, 5, 4, 7)
    transpose_docs(4, 2)
    sib[4].wait_recv()
    sib[5].wait_recv()
    scores(0, 4, 0, 4, 6)
    scores(4, 2, 1, 0, 6)

    q_far[0].wait_recv()
    q_far[1].wait_recv()
    sib[6] = to_sibling(6)
    q_far[2].wait_recv()
    q_far[3].wait_recv()
    sib[7] = to_sibling(7)
    for copy in d_far:
        copy.wait_recv()
    transpose_docs(6, 2)
    scores(6, 2, 2, 0, 6)
    sib[6].wait_recv()
    sib[7].wait_recv()
    scores(0, 4, 0, 6, 8)
    scores(4, 2, 1, 6, 8)
    scores(6, 2, 2, 6, 8)

    top = jnp.maximum(jnp.maximum(mst[0], mst[1]), mst[2])
    total = sum(sst[b] * jnp.exp(mst[b] - top) for b in range(3))
    local = top + jnp.log(jnp.maximum(total, 1e-37))
    places = []
    for k, (dx, dy) in enumerate(OFFSETS):
        for dc in range(2):
            place = pl.ds(pl.multiple_of(dev_at(dx, dy, dc) * rows, rows), rows)
            places.append(place)
            n = k * 2 + dc
            lsend[:, place] = local[:, n * rows : (n + 1) * rows]
    lse_copies = [send(lsend, lbuf.at[s], q_peer(*dev_offsets[s])) for s in range(1, 16)]
    lbuf[0] = lsend[...]
    for copy in lse_copies:
        copy.wait_recv()
    every = [lbuf[s] for s in range(16)]
    top = every[0]
    for e in every[1:]:
        top = jnp.maximum(top, e)
    total = sum(jnp.exp(e - top) for e in every)
    lsef[...] = top + jnp.log(total)
    for n, place in enumerate(places):
        lrel[:, n * rows : (n + 1) * rows] = lsef[:, place]
    for b in range(3):
        sst[b] = jnp.exp(mst[b] - lrel[...])

    def grads(g, carry):
        cols = pl.ds(pl.multiple_of(g * 2 * rows, 2 * rows), 2 * rows)
        pos, weight = labs[0:1, cols], labs[2:3, cols]
        for k in range(8):
            scale = sst[0 if k < 4 else 1 if k < 6 else 2, :, cols]
            hit = jnp.where(lane == pos - bases(k), jnp.float32(1), jnp.float32(0))
            prob = st[k * rows : (k + 1) * rows, cols] * scale
            gt[k * rows : (k + 1) * rows, cols] = (weight * (prob - hit)).astype(bf16)
        return carry

    lax.fori_loop(0, 8, grads, 0)

    def doc_terms(first):
        def body(j, carry):
            cols = pl.ds(pl.multiple_of(j * 256, 256), 256)
            v = jnp.dot(gt[first * rows : (first + 2) * rows, :], qbuf[:, cols], preferred_element_type=f32).astype(bf16)
            gdp[first, :, cols] = v[:rows]
            gdp[first + 1, :, cols] = v[rows:]
            return carry

        lax.fori_loop(0, 4, body, 0)

    cores = {}

    def query_terms(k):
        def body(j, carry):
            part = pl.ds(pl.multiple_of(j * 512, 512), 512)
            v = jnp.dot(dt[part, :], gt[:, k * 2 * rows : (k + 1) * 2 * rows], preferred_element_type=f32).astype(bf16)
            gqp[k, 0, part, :] = v[:, :rows]
            gqp[k, 1, part, :] = v[:, rows:]
            return carry

        lax.fori_loop(0, 2, body, 0)
        cores[k] = send(gqp.at[k, 1], cbuf.at[k], q_peer(0, 0, 1))

    def both_cores(k):
        cores[k].wait_recv()
        sbuf[k] = (gqp[k, 0].astype(f32) + cbuf[k].astype(f32)).astype(bf16)

    def far_terms(src, fold, peer, dx, far, h):
        return [
            send(src.at[far, pl.ds(0, h), :], fold.at[dx, 0], peer(0, 1)),
            send(src.at[far, pl.ds(h, h), :], fold.at[dx, 1], peer(0, 3)),
        ]

    def near_plus(src, ring, peer, dx, plus, h):
        return [send(src.at[plus, pl.ds(h, h), :], ring.at[dx, 0, pl.ds(h, h), :], peer(0, 1))]

    def near_minus(src, ring, peer, dx, minus, h):
        return [send(src.at[minus, pl.ds(0, h), :], ring.at[dx, 1, pl.ds(0, h), :], peer(0, 3))]

    def merged(src, fold, ring, peer, dx, plus, minus, h, waits):
        waits[0].wait_recv()
        src[plus, 0:h, :] = (src[plus, 0:h, :].astype(f32) + fold[dx, 0].astype(f32)).astype(bf16)
        a = send(src.at[plus, pl.ds(0, h), :], ring.at[dx, 0, pl.ds(0, h), :], peer(0, 1))
        waits[1].wait_recv()
        src[minus, h : 2 * h, :] = (src[minus, h : 2 * h, :].astype(f32) + fold[dx, 1].astype(f32)).astype(bf16)
        b = send(src.at[minus, pl.ds(h, h), :], ring.at[dx, 1, pl.ds(h, h), :], peer(0, 3))
        return [a, b]

    def ring_sum(src, ring, dx, own, waits):
        for copy in waits:
            copy.wait_recv()
        return src[own].astype(f32) + ring[dx, 0].astype(f32) + ring[dx, 1].astype(f32)

    hd, hq = half, width // 2
    doc_terms(6)
    d_fold1 = far_terms(gdp, dfold, d_peer, 1, 7, hd)
    d_fold0 = far_terms(gdp, dfold, d_peer, 0, 6, hd)
    query_terms(7)
    doc_terms(4)
    d_ring1 = near_plus(gdp, dring, d_peer, 1, 4, hd) + near_minus(gdp, dring, d_peer, 1, 5, hd)
    query_terms(4)
    query_terms(5)
    both_cores(7)
    q_fold1 = far_terms(sbuf, qfold, q_peer, 1, 7, hq)
    query_terms(6)
    both_cores(4)
    both_cores(5)
    q_ring1 = near_plus(sbuf, qring, q_peer, 1, 4, hq) + near_minus(sbuf, qring, q_peer, 1, 5, hq)
    d_ring1 += merged(gdp, dfold, dring, d_peer, 1, 4, 5, hd, d_fold1)
    both_cores(6)
    q_fold0 = far_terms(sbuf, qfold, q_peer, 0, 6, hq)
    query_terms(3)
    query_terms(1)
    query_terms(2)
    q_ring1 += merged(sbuf, qfold, qring, q_peer, 1, 4, 5, hq, q_fold1)
    doc_terms(2)
    doc_terms(0)
    d_ring0 = near_plus(gdp, dring, d_peer, 0, 1, hd) + near_minus(gdp, dring, d_peer, 0, 2, hd)
    both_cores(1)
    both_cores(2)
    q_ring0 = near_plus(sbuf, qring, q_peer, 0, 1, hq) + near_minus(sbuf, qring, q_peer, 0, 2, hq)
    query_terms(0)
    d_ring0 += merged(gdp, dfold, dring, d_peer, 0, 1, 2, hd, d_fold0)
    q_ring0 += merged(sbuf, qfold, qring, q_peer, 0, 1, 2, hq, q_fold0)
    both_cores(3)
    both_cores(0)
    dx_buf[0] = ring_sum(gdp, dring, 1, 3, d_ring1).astype(bf16)
    d_across = send(dx_buf.at[0], dx_buf.at[1], d_peer(1, 0))
    qx[0] = ring_sum(sbuf, qring, 1, 3, q_ring1).astype(bf16)
    q_across = send(qx.at[0], qx.at[1], q_peer(1, 0))

    def backward(g_unit, low, out):
        span = slice(low, low + rows)
        uu, nn = unit[span, :], normed[span, :]
        g = ((g_unit - uu * jnp.sum(uu * g_unit, axis=1, keepdims=True)) * inv[span, :]).astype(bf16)
        ge[span, :] = g
        gn = lax.dot_general(g, proj[...], NT, preferred_element_type=f32)
        scaled = gn * gain[...]
        out[...] = (
            recip[span, :]
            * (scaled - jnp.mean(scaled, axis=1, keepdims=True) - nn * jnp.mean(scaled * nn, axis=1, keepdims=True))
        ).astype(bf16)
        return jnp.sum(gn * nn, axis=0, keepdims=True), jnp.sum(gn, axis=0, keepdims=True)

    g_doc = ring_sum(gdp, dring, 0, 0, d_ring0)
    d_across.wait_recv()
    gain_d, bias_d = backward(logit_scale * (g_doc + dx_buf[1].astype(f32)), rows, dd)
    g_query = ring_sum(sbuf, qring, 0, 0, q_ring0)
    q_across.wait_recv()
    gain_q, bias_q = backward(logit_scale * (g_query + qx[1].astype(f32)).T, 0, dq)

    gb[0:1, :] = gain_d + gain_q
    gb[1:2, :] = bias_d + bias_q
    gb_copies = [send(gb, gba.at[dev], q_peer(*o)) for o in dev_offsets[1:]]
    gba[dev] = gb[...]

    def head(n, carry):
        v = jnp.dot(
            out_t[pl.ds(pl.multiple_of(n * rows, rows), rows), :], ge[...], preferred_element_type=f32
        ).astype(bf16)
        for j in range(8):
            for h in range(2):
                hp[h, j % 2, j // 2, n] = v[h * half : (h + 1) * half, j * rows : (j + 1) * rows]
        return carry

    lax.fori_loop(0, 8, head, 0)
    head_core = send(hp.at[1 - core], hc, q_peer(0, 0, 1))
    head_core.wait_recv()

    def add_cores(n, carry):
        for a in range(2):
            hs[a, n] = (hp[core, a, n].astype(f32) + hc[a, n].astype(f32)).astype(bf16)
        return carry

    lax.fori_loop(0, 4, add_cores, 0)

    first = []
    for s in range(1, 4):
        zz, yy = lax.rem(z + s, 4), lax.rem(y + s, 4)
        first.append(send(hs.at[0, :, pl.ds(zz * 2, 2)], hz1.at[s - 1], d_peer(0, s)))
        first.append(send(hs.at[1, yy], hy1.at[s - 1], q_peer(0, s)))

    for copy in gb_copies:
        copy.wait_recv()
    acc = gba[0]
    for n in range(1, 16):
        acc = acc + gba[n]
    gbb[pb] = acc
    gb_copies = [send(gbb.at[pb], gbb.at[pb], d_peer(*o)) for o in pb_offsets[1:]]

    for copy in first:
        copy.wait_recv()
    h0[...] = (hs[0, :, pl.ds(z * 2, 2)].astype(f32) + sum(hz1[n].astype(f32) for n in range(3))).astype(bf16)
    h1[...] = (hs[1, y].astype(f32) + sum(hy1[n].astype(f32) for n in range(3))).astype(bf16)
    second = []
    for s in range(1, 4):
        zz, yy = lax.rem(z + s, 4), lax.rem(y + s, 4)
        second.append(send(h0.at[yy], hy2.at[s - 1], q_peer(0, s)))
        second.append(send(h1.at[pl.ds(zz * 2, 2)], hz2.at[s - 1], d_peer(0, s)))
    for copy in second:
        copy.wait_recv()
    hx[0] = (h0[y].astype(f32) + sum(hy2[n].astype(f32) for n in range(3))).astype(bf16)
    hx[1] = (h1[pl.ds(z * 2, 2)].astype(f32) + sum(hz2[n].astype(f32) for n in range(3))).astype(bf16)
    third = []
    for s, (dh_, dl) in enumerate(((0, 1), (1, 0), (1, 1))):
        src = hx.at[lax.rem(xh + dh_, 2), lax.rem(xl + dl, 2)]
        third.append(send(src, hx3.at[s], (pb_at(dl, 0), dev_at(dh_, 0, 0))))
    for copy in third:
        copy.wait_recv()
    hf[...] = hx[xh, xl].astype(f32) + sum(hx3[n].astype(f32) for n in range(3))
    last = send(hf, hfs, q_peer(0, 0, 1))
    last.wait_recv()

    def mine(v):
        return jnp.where(core == 0, v[:, :half], v[:, half:])

    dproj[pl.ds(core * half, half), :] = mine(hf[...])
    dproj[pl.ds((1 - core) * half, half), :] = mine(hfs[...])

    for copy in gb_copies:
        copy.wait_recv()
    acc = gbb[0]
    for n in range(1, 8):
        acc = acc + gbb[n]
    dgb[...] = acc

    for copy in started:
        copy.wait_send()


def per_device(
    q_hidden, d_hidden, positive, query_part, doc_part, loss_weight, norm_gain, norm_bias, proj
):
    lab_q = jnp.zeros((8, rows), f32)
    lab_q = lab_q.at[0].set(positive.astype(f32)).at[1].set(query_part.astype(f32)).at[2].set(loss_weight.astype(f32))
    lab_d = jnp.broadcast_to(doc_part.astype(f32)[None, :], (8, rows))
    vmem = pl.BlockSpec(memory_space=pltpu.VMEM)
    V = pltpu.VMEM
    e = width
    scratch = [
        V((e, e), bf16),
        V((16 * rows, e), bf16),
        V((8 * rows, e), bf16),
        V((e, 8 * rows), bf16),
        V((8 * rows, 16 * rows), f32),
        V((8 * rows, 16 * rows), bf16),
        V((2 * rows, e), f32),
        V((2 * rows, e), f32),
        V((2 * rows, 1), f32),
        V((2 * rows, 1), f32),
        V((e, 2 * rows), bf16),
        V((8, 16 * rows), f32),
        V((8, 8, rows), f32),
        V((8 * rows, rows), f32),
        V((3, 1, 16 * rows), f32),
        V((3, 1, 16 * rows), f32),
        V((1, 16 * rows), f32),
        V((16, 1, 16 * rows), f32),
        V((1, 16 * rows), f32),
        V((1, 16 * rows), f32),
        V((8, 2, e, rows), bf16),
        V((8, e, rows), bf16),
        V((8, e, rows), bf16),
        V((2, 2, e // 2, rows), bf16),
        V((2, 2, e, rows), bf16),
        V((2, e, rows), bf16),
        V((8, rows, e), bf16),
        V((2, 2, half, e), bf16),
        V((2, 2, rows, e), bf16),
        V((2, rows, e), bf16),
        V((2 * rows, e), bf16),
        V((2, 2, 4, 8, half, rows), bf16),
        V((2, 4, 8, half, rows), bf16),
        V((2, 4, 8, half, rows), bf16),
        V((3, 4, 2, half, rows), bf16),
        V((3, 8, half, rows), bf16),
        V((4, 2, half, rows), bf16),
        V((8, half, rows), bf16),
        V((3, 2, half, rows), bf16),
        V((3, 2, half, rows), bf16),
        V((2, 2, half, rows), bf16),
        V((3, half, rows), bf16),
        V((half, rows), f32),
        V((half, rows), f32),
        V((2, e), f32),
        V((16, 2, e), f32),
        V((8, 2, e), f32),
        pltpu.SemaphoreType.DMA((copies,)),
        pltpu.SemaphoreType.DMA((copies,)),
        pltpu.SemaphoreType.DMA,
    ]
    dq, dd, d_proj, dgb = pl.pallas_call(
        kernel,
        out_shape=(
            jax.ShapeDtypeStruct((rows, e), bf16),
            jax.ShapeDtypeStruct((rows, e), bf16),
            jax.ShapeDtypeStruct((rows, half), f32),
            jax.ShapeDtypeStruct((2, e), f32),
        ),
        in_specs=[vmem] * 6 + [pl.BlockSpec(memory_space=pl.ANY)],
        out_specs=(vmem,) * 4,
        scratch_shapes=scratch,
        compiler_params=pltpu.CompilerParams(
            collective_id=0, has_side_effects=True, vmem_limit_bytes=60 * 1024 * 1024
        ),
        cost_estimate=pl.CostEstimate(flops=16_000_000_000, bytes_accessed=5_000_000, transcendentals=2_100_000),
    )(q_hidden, d_hidden, lab_q, lab_d, norm_gain.reshape(1, e), norm_bias.reshape(1, e), proj)
    return dq, dd, d_proj, dgb[0], dgb[1]


def solution(mesh):
    placed = (
        P(("pb", "dev"), None),
        P(("dev", "pb"), None),
        P(("pb", "dev")),
        P(("pb", "dev")),
        P(("dev", "pb")),
        P(("pb", "dev")),
        P(),
        P(),
        P(),
    )
    return jax.shard_map(
        per_device,
        mesh=mesh,
        in_specs=placed,
        out_specs=(P(("pb", "dev"), None), P(("dev", "pb"), None), P("pb", "dev"), P(), P()),
        check_vma=False,
    )
```

```python
import jax
import jax.numpy as jnp
from jax import lax
from jax.experimental import pallas as pl
from jax.experimental.pallas import tpu as pltpu
from jax.sharding import PartitionSpec as P

logit_scale = 100.0
f32, bf16 = jnp.float32, jnp.bfloat16
MESH = pl.DeviceIdType.MESH
rows, width = 128, 1024
half = rows // 2
copies = 160
OFFSETS = ((0, 0), (1, 0), (0, 1), (0, 3), (0, 2), (1, 2), (1, 1), (1, 3))
NT = (((1,), (1,)), ((), ()))


def kernel(
    qh_hbm, dh_hbm, pos_hbm, qpart_hbm, weight_hbm, dpart_hbm, gain_hbm, bias_hbm, proj_hbm,
    dq, dd, dproj, dgain, dbias,
    qh, dh, pos_in, qpart_in, weight_in, dpart_in, gain, bias,
    proj, qbuf, dbuf, dt, st, gt, unit, normed, recip, inv, out_t, lab_q, lab_d, labs, dlab, dcol, mst, sst, lsend, lbuf,
    lsef, lrel, gqp, cbuf, sbuf, qfold, qring, qx, gdp, dfold, dring, dx_buf,
    ge, hp, hc, hs, hz1, hy1, h0, h1, hy2, hz2, hx, hx3, gb, gba, gbb,
    send_sem, recv_sem, local_sem,
):
    pb, dev = lax.axis_index("pb"), lax.axis_index("dev")
    z, xl = pb // 2, lax.rem(pb, 2)
    y, xh, core = dev // 4, lax.rem(dev // 2, 2), lax.rem(dev, 2)

    def q_peer(dx, dy, dc=0):
        return (z * 2 + lax.rem(xl + dx, 2), lax.rem(y + dy, 4) * 4 + xh * 2 + lax.rem(core + dc, 2))

    def d_peer(dx, dz):
        return (lax.rem(z + dz, 4) * 2 + lax.rem(xl + dx, 2), y * 4 + lax.rem(xh + dx, 2) * 2 + core)

    def x_peer(dh, dl):
        return (z * 2 + lax.rem(xl + dl, 2), y * 4 + lax.rem(xh + dh, 2) * 2 + core)

    started = []

    def send(src, dst, peer):
        n = len(started)
        copy = pltpu.make_async_remote_copy(
            src_ref=src, dst_ref=dst, send_sem=send_sem.at[n], recv_sem=recv_sem.at[n],
            device_id=peer, device_id_type=MESH,
        )
        copy.start()
        started.append(copy)
        return copy

    def arrive(*copies):
        for copy in copies:
            copy.wait_recv()

    q_offsets = [(dx, dy, dc) for dx in range(2) for dy in range(4) for dc in range(2)]
    d_offsets = [(dx, dz) for dx in range(2) for dz in range(4)]

    loads = []
    for n, (src, dst) in enumerate((
        (qh_hbm, qh), (dh_hbm, dh), (proj_hbm, proj), (gain_hbm, gain), (bias_hbm, bias),
        (pos_hbm, pos_in), (qpart_hbm, qpart_in), (weight_hbm, weight_in), (dpart_hbm, dpart_in),
    )):
        loads.append(pltpu.make_async_copy(src, dst, local_sem.at[n]))
        loads[-1].start()
    barrier = pltpu.get_barrier_semaphore()
    peers = [q_peer(*o) for o in q_offsets[1:]] + [d_peer(*o) for o in d_offsets[1:]] + [x_peer(1, 0)]
    for peer in peers:
        pl.semaphore_signal(barrier, inc=1, device_id=peer, device_id_type=MESH)

    for n in (0, 1, 3, 4, 5, 6, 7, 8):
        loads[n].wait()
    lab_q[...] = jnp.zeros((8, rows), f32)
    lab_q[0:1, :] = pos_in[...].astype(f32)
    lab_q[1:2, :] = qpart_in[...].astype(f32)
    lab_q[2:3, :] = weight_in[...].astype(f32)
    lab_d[...] = jnp.broadcast_to(dpart_in[...].astype(f32), (8, rows))
    values = jnp.concatenate([qh[...], dh[...]], axis=0).astype(f32)
    centred = values - jnp.mean(values, axis=1, keepdims=True)
    r = lax.rsqrt(jnp.mean(centred * centred, axis=1, keepdims=True) + 1e-05)
    norm = centred * r
    recip[...] = r
    normed[...] = norm
    normal_out = (norm * gain[...] + bias[...]).astype(bf16)
    loads[2].wait()
    pl.semaphore_wait(barrier, len(peers))

    block = 8 * rows

    def q_at(core_index, k, offset=0):
        return pl.multiple_of(core_index * block + k * rows + offset, half)

    lab_copies = []
    for dx, dy, dc in q_offsets[1:]:
        k = OFFSETS.index((dx, (4 - dy) % 4))
        dst = labs.at[:, pl.ds(pl.multiple_of(core * block + k * rows, rows), rows)]
        lab_copies.append(send(lab_q, dst, q_peer(dx, dy, dc)))
    for dx, dz in d_offsets[1:]:
        lab_copies.append(send(lab_d, dlab.at[OFFSETS.index((dx, (4 - dz) % 4))], d_peer(dx, dz)))
    labs[:, pl.ds(pl.multiple_of(core * block, rows), rows)] = lab_q[...]
    dlab[0] = lab_d[...]

    embed = jnp.dot(normal_out, proj[...], preferred_element_type=f32)
    i = lax.rsqrt(jnp.sum(embed * embed, axis=1, keepdims=True) + 1e-06)
    inv[...] = i
    u = embed * i
    unit[...] = u
    qbuf[pl.ds(q_at(core, 0), rows), :] = u[:rows].astype(bf16)
    dbuf[0:rows, :] = u[rows:].astype(bf16)

    def q_half(k, h):
        return qbuf.at[pl.ds(q_at(core, k, h * half), half), :]

    def d_half(k, h):
        return dbuf.at[pl.ds(k * rows + h * half, half), :]

    def to_sibling(k):
        part = qbuf.at[pl.ds(pl.multiple_of(core * block + k * rows, rows), rows), :]
        return send(part, part, q_peer(0, 0, 1))

    q_got, d_got, sib = {}, {}, {}

    def hop(part, got, peer, k, h, to, way):
        got[to, h] = send(part(k, h), part(to, h), peer(1, 0) if way == 0 else peer(0, way))

    towers = ((q_half, q_got, q_peer), (d_half, d_got, d_peer))
    for h in range(2):
        for tower in towers:
            hop(*tower, 0, h, 3, 1)
            hop(*tower, 0, 1 - h, 2, 3)
            hop(*tower, 0, h, 1, 0)
    sib[0] = to_sibling(0)
    out_t[...] = normal_out.T
    for tower in towers:
        arrive(tower[1][3, 0])
        hop(*tower, 3, 0, 4, 1)
        arrive(tower[1][2, 1])
        hop(*tower, 2, 1, 4, 3)
    for tower in towers:
        arrive(tower[1][1, 0])
        hop(*tower, 1, 0, 7, 1)
    for tower in towers:
        arrive(tower[1][1, 1])
        hop(*tower, 1, 1, 6, 3)
        hop(*tower, 1, 1, 7, 1)
        hop(*tower, 1, 0, 6, 3)
    sib[1] = to_sibling(1)
    arrive(q_got[3, 1], q_got[2, 0])
    sib[2], sib[3] = to_sibling(2), to_sibling(3)
    arrive(*lab_copies)
    arrive(d_got[3, 1], d_got[2, 0])

    for k in range(8):
        dcol[k * rows : (k + 1) * rows, :] = jnp.broadcast_to(dlab[k, 0:1, :], (rows, rows)).T

    def transpose_docs(first, count):
        for k in range(first, first + count):
            dt[:, k * rows : (k + 1) * rows] = dbuf[k * rows : (k + 1) * rows, :].T

    lane = lax.broadcasted_iota(jnp.int32, (rows, 2 * rows), 0).astype(f32)

    def bases(k):
        to_pb, to_dev = d_peer(*OFFSETS[k])
        return ((to_dev * 8 + to_pb) * rows).astype(f32)

    def pair_cols(core_index, m):
        return pl.ds(pl.multiple_of(core_index * block + m * 2 * rows, 2 * rows), 2 * rows)

    def score(first, count, piece, cols):
        s = logit_scale * lax.dot_general(
            dbuf[first * rows : (first + count) * rows, :], qbuf[cols, :], NT, preferred_element_type=f32
        )
        pos, part = labs[0:1, cols], labs[1:2, cols]
        masked = []
        for n in range(count):
            k = first + n
            col = dcol[k * rows : (k + 1) * rows, :]
            valid = jnp.logical_or(part != jnp.concatenate([col, col], axis=1), lane == pos - bases(k))
            masked.append(jnp.where(valid, s[n * rows : (n + 1) * rows], jnp.float32(-1e30)))
        top = jnp.full((1, 2 * rows), -1e4, f32)
        for m in masked:
            top = jnp.maximum(top, jnp.max(m, axis=0, keepdims=True))
        total = jnp.zeros((1, 2 * rows), f32)
        for n, m in enumerate(masked):
            p = jnp.exp(m - top)
            total = total + jnp.sum(p, axis=0, keepdims=True)
            st[(first + n) * rows : (first + n + 1) * rows, cols] = p
        mst[piece, :, cols] = top
        sst[piece, :, cols] = total

    pieces = ((0, 4), (4, 2), (6, 2))

    def scores(piece, pairs):
        low, step, count = pairs

        def body(n, carry):
            m, c = low + step * (n // 2), lax.rem(n, 2)
            score(*pieces[piece], piece, pair_cols(c, m))
            return carry

        lax.fori_loop(0, 2 * count, body, 0)

    transpose_docs(0, 4)
    arrive(sib[0], sib[1], sib[2], sib[3])
    scores(0, (0, 1, 2))

    for tower in towers:
        arrive(tower[1][7, 0])
        hop(*tower, 7, 0, 5, 1)
        arrive(tower[1][6, 1])
        hop(*tower, 6, 1, 5, 3)
    arrive(q_got[7, 1], q_got[6, 0])
    sib[6], sib[7] = to_sibling(6), to_sibling(7)
    arrive(q_got[4, 0], q_got[4, 1])
    sib[4] = to_sibling(4)
    arrive(d_got[7, 1], d_got[6, 0], d_got[4, 0], d_got[4, 1])
    transpose_docs(6, 2)
    transpose_docs(4, 1)
    scores(2, (0, 1, 2))
    arrive(sib[6], sib[7])
    scores(0, (3, 1, 1))
    scores(2, (3, 1, 1))

    arrive(q_got[5, 0], q_got[5, 1])
    sib[5] = to_sibling(5)
    arrive(d_got[5, 0], d_got[5, 1])
    transpose_docs(5, 1)
    scores(1, (0, 1, 2))
    scores(1, (3, 1, 1))
    arrive(sib[4], sib[5])
    scores(0, (2, 1, 1))
    scores(1, (2, 1, 1))
    scores(2, (2, 1, 1))

    top = jnp.maximum(jnp.maximum(mst[0], mst[1]), mst[2])
    total = sum(sst[b] * jnp.exp(mst[b] - top) for b in range(3))
    local = top + jnp.log(jnp.maximum(total, 1e-37))
    places = []
    for n in range(16):
        c, (dx, dy) = n // 8, OFFSETS[n % 8]
        place = c * block + (lax.rem(y + dy, 4) * 2 + lax.rem(xl + dx, 2)) * rows
        places.append(pl.ds(pl.multiple_of(place, rows), rows))
        lsend[:, places[-1]] = local[:, n * rows : (n + 1) * rows]
    lse_copies = [send(lsend, lbuf.at[s], q_peer(*q_offsets[s])) for s in range(1, 16)]
    lbuf[0] = lsend[...]
    arrive(*lse_copies)
    every = [lbuf[s] for s in range(16)]
    top = every[0]
    for e in every[1:]:
        top = jnp.maximum(top, e)
    total = sum(jnp.exp(e - top) for e in every)
    lsef[...] = top + jnp.log(total)
    for n, place in enumerate(places):
        lrel[:, n * rows : (n + 1) * rows] = lsef[:, place]
    for b in range(3):
        sst[b] = jnp.exp(mst[b] - lrel[...])

    def grads(g, carry):
        cols = pl.ds(pl.multiple_of(g * 2 * rows, 2 * rows), 2 * rows)
        pos, weight = labs[0:1, cols], labs[2:3, cols]
        for k in range(8):
            scale = sst[0 if k < 4 else 1 if k < 6 else 2, :, cols]
            hit = jnp.where(lane == pos - bases(k), jnp.float32(1), jnp.float32(0))
            prob = st[k * rows : (k + 1) * rows, cols] * scale
            gt[k * rows : (k + 1) * rows, cols] = (weight * (prob - hit)).astype(bf16)
        return carry

    lax.fori_loop(0, 8, grads, 0)

    def doc_terms(m):
        def body(j, carry):
            cols = pl.ds(pl.multiple_of(j * 256, 256), 256)
            v = jnp.dot(
                gt[2 * m * rows : 2 * (m + 1) * rows, :], qbuf[:, cols], preferred_element_type=f32
            ).astype(bf16)
            gdp[2 * m, :, cols] = v[:rows]
            gdp[2 * m + 1, :, cols] = v[rows:]
            return carry

        lax.fori_loop(0, 4, body, 0)

    cores = {}

    def query_terms(m, other):
        cols = pair_cols(1 - core if other else core, m)

        def body(j, carry):
            part = pl.ds(pl.multiple_of(j * 512, 512), 512)
            v = jnp.dot(dt[part, :], gt[:, cols], preferred_element_type=f32).astype(bf16)
            gqp[other, 2 * m, part, :] = v[:, :rows]
            gqp[other, 2 * m + 1, part, :] = v[:, rows:]
            return carry

        lax.fori_loop(0, 2, body, 0)
        if other:
            span = pl.ds(2 * m, 2)
            cores[m] = send(gqp.at[1, span], cbuf.at[span], q_peer(0, 0, 1))

    def both_cores(k):
        if k // 2 in cores:
            arrive(cores.pop(k // 2))
        sbuf[k] = (gqp[0, k].astype(f32) + cbuf[k].astype(f32)).astype(bf16)

    slots = ((0, 2, 3, 4), (1, 6, 7, 5))

    def far_terms(src, fold, ring, peer, h, dx):
        far = slots[dx][3]
        return [
            send(src.at[far, pl.ds(0, h), :], fold.at[dx, 0], peer(0, 1)),
            send(src.at[far, pl.ds(h, h), :], fold.at[dx, 1], peer(0, 3)),
        ]

    def near_terms(src, fold, ring, peer, h, dx):
        _, plus, minus, _ = slots[dx]
        return [
            send(src.at[plus, pl.ds(h, h), :], ring.at[dx, 0, pl.ds(h, h), :], peer(0, 1)),
            send(src.at[minus, pl.ds(0, h), :], ring.at[dx, 1, pl.ds(0, h), :], peer(0, 3)),
        ]

    def merged(src, fold, ring, peer, h, dx, waits):
        _, plus, minus, _ = slots[dx]
        arrive(waits[0])
        src[plus, 0:h, :] = (src[plus, 0:h, :].astype(f32) + fold[dx, 0].astype(f32)).astype(bf16)
        a = send(src.at[plus, pl.ds(0, h), :], ring.at[dx, 0, pl.ds(0, h), :], peer(0, 1))
        arrive(waits[1])
        src[minus, h : 2 * h, :] = (src[minus, h : 2 * h, :].astype(f32) + fold[dx, 1].astype(f32)).astype(bf16)
        b = send(src.at[minus, pl.ds(h, h), :], ring.at[dx, 1, pl.ds(h, h), :], peer(0, 3))
        return [a, b]

    def ring_sum(src, ring, dx, waits):
        arrive(*waits)
        return src[dx].astype(f32) + ring[dx, 0].astype(f32) + ring[dx, 1].astype(f32)

    D = (gdp, dfold, dring, d_peer, half)
    Q = (sbuf, qfold, qring, q_peer, width // 2)
    query_terms(2, 1)
    query_terms(2, 0)
    query_terms(3, 1)
    doc_terms(2)
    d_fold1 = far_terms(*D, 1)
    both_cores(5)
    q_fold1 = far_terms(*Q, 1)
    query_terms(3, 0)
    both_cores(6)
    both_cores(7)
    q_ring1 = near_terms(*Q, 1)
    doc_terms(3)
    d_ring1 = near_terms(*D, 1)
    both_cores(4)
    query_terms(1, 1)
    query_terms(0, 1)
    query_terms(1, 0)
    d_ring1 += merged(*D, 1, d_fold1)
    d_fold0 = far_terms(*D, 0)
    q_ring1 += merged(*Q, 1, q_fold1)
    q_fold0 = far_terms(*Q, 0)
    doc_terms(1)
    d_ring0 = near_terms(*D, 0)
    both_cores(2)
    both_cores(3)
    q_ring0 = near_terms(*Q, 0)
    query_terms(0, 0)
    doc_terms(0)
    both_cores(1)
    both_cores(0)
    dx_buf[0] = ring_sum(gdp, dring, 1, d_ring1).astype(bf16)
    d_across = send(dx_buf.at[0], dx_buf.at[1], d_peer(1, 0))
    qx[0] = ring_sum(sbuf, qring, 1, q_ring1).astype(bf16)
    q_across = send(qx.at[0], qx.at[1], q_peer(1, 0))
    d_ring0 += merged(*D, 0, d_fold0)
    q_ring0 += merged(*Q, 0, q_fold0)

    def backward(g_unit, low, out):
        span = slice(low, low + rows)
        uu, nn = unit[span, :], normed[span, :]
        g = ((g_unit - uu * jnp.sum(uu * g_unit, axis=1, keepdims=True)) * inv[span, :]).astype(bf16)
        ge[span, :] = g
        gn = lax.dot_general(g, proj[...], NT, preferred_element_type=f32)
        scaled = gn * gain[...]
        out[...] = (
            recip[span, :]
            * (scaled - jnp.mean(scaled, axis=1, keepdims=True) - nn * jnp.mean(scaled * nn, axis=1, keepdims=True))
        ).astype(bf16)
        return jnp.sum(gn * nn, axis=0, keepdims=True), jnp.sum(gn, axis=0, keepdims=True)

    g_doc = ring_sum(gdp, dring, 0, d_ring0)
    arrive(d_across)
    g_doc = logit_scale * (g_doc + dx_buf[1].astype(f32))
    g_query = ring_sum(sbuf, qring, 0, q_ring0)
    arrive(q_across)
    gain_d, bias_d = backward(g_doc, rows, dd)
    gain_q, bias_q = backward(logit_scale * (g_query + qx[1].astype(f32)).T, 0, dq)

    gb[0:1, :] = gain_d + gain_q
    gb[1:2, :] = bias_d + bias_q
    order = (y * 2 + xl) * 2 + core
    gb_copies = [send(gb, gba.at[order], q_peer(*o)) for o in q_offsets[1:]]
    gba[order] = gb[...]

    left = lax.broadcasted_iota(jnp.int32, (half, rows), 1) < half

    def head(n, carry):
        for a in range(2):
            v = jnp.dot(
                out_t[pl.ds(pl.multiple_of((2 * n + a) * rows, rows), rows), :], ge[...], preferred_element_type=f32
            )
            for j in range(8):
                upper, lower = v[:half, j * rows : (j + 1) * rows], v[half:, j * rows : (j + 1) * rows]
                hp[0, a, j % 2, j // 2, n] = jnp.where(left, upper, pltpu.roll(lower, half, 1)).astype(bf16)
                hp[1, a, j % 2, j // 2, n] = jnp.where(left, pltpu.roll(upper, half, 1), lower).astype(bf16)
        return carry

    lax.fori_loop(0, 4, head, 0)
    head_core = [send(hp.at[1 - core, a], hc.at[a], q_peer(0, 0, 1)) for a in range(2)]
    first = []
    for a in range(2):
        arrive(head_core[a])

        def add_cores(n, carry):
            for b in range(2):
                hs[a, b, n] = (hp[core, a, b, n].astype(f32) + hc[a, b, n].astype(f32)).astype(bf16)
            return carry

        lax.fori_loop(0, 4, add_cores, 0)
        for s in range(1, 4):
            zz, yy = lax.rem(z + s, 4), lax.rem(y + s, 4)
            if a == 0:
                first.append(send(hs.at[0, :, :, zz], hz1.at[s - 1], d_peer(0, s)))
            else:
                first.append(send(hs.at[1, :, yy], hy1.at[s - 1], q_peer(0, s)))

    arrive(*gb_copies)
    acc = gba[0]
    for n in range(1, 16):
        acc = acc + gba[n]
    order = z * 2 + xh
    gbb[order] = acc
    gb_copies = [send(gbb.at[order], gbb.at[order], d_peer(*o)) for o in d_offsets[1:]]

    def total_of(own, got):
        return own.astype(f32) + sum(got[n].astype(f32) for n in range(3))

    arrive(*first[:3])
    h0[...] = total_of(hs[0, :, :, z], hz1).astype(bf16)
    second = [send(h0.at[:, lax.rem(y + s, 4)], hy2.at[s - 1], q_peer(0, s)) for s in range(1, 4)]
    arrive(*first[3:])
    h1[...] = total_of(hs[1, :, y], hy1).astype(bf16)
    second += [send(h1.at[:, lax.rem(z + s, 4)], hz2.at[s - 1], d_peer(0, s)) for s in range(1, 4)]
    arrive(*second)
    hx[0] = total_of(h0[:, y], hy2).astype(bf16)
    hx[1] = total_of(h1[:, z], hz2).astype(bf16)
    third = []
    for s, (sh, sl) in enumerate(((0, 1), (1, 0), (1, 1))):
        src = hx.at[lax.rem(xl + sl, 2), lax.rem(xh + sh, 2)]
        third.append(send(src, hx3.at[s], x_peer(sh, sl)))
    arrive(*third)
    final = total_of(hx[xl, xh], hx3)
    dproj[:, 0:half] = final[:, :half].T
    dproj[:, half:rows] = final[:, half:].T

    arrive(*gb_copies)
    acc = gbb[0]
    for n in range(1, 8):
        acc = acc + gbb[n]
    dgain[...] = acc[0:1]
    dbias[...] = acc[1:2]

    for copy in started:
        copy.wait_send()


def hand_over(*refs):
    for src, dst in zip(refs[:5], refs[5:]):
        dst[...] = src[...]


def per_device(
    q_hidden, d_hidden, positive, query_part, doc_part, loss_weight, norm_gain, norm_bias, proj
):
    vmem = pl.BlockSpec(memory_space=pltpu.VMEM)
    V = pltpu.VMEM
    e = width
    scratch = [
        V((rows, e), bf16),
        V((rows, e), bf16),
        V((1, rows), jnp.int32),
        V((1, rows), jnp.int32),
        V((1, rows), bf16),
        V((1, rows), jnp.int32),
        V((1, e), f32),
        V((1, e), f32),
        V((e, e), bf16),
        V((16 * rows, e), bf16),
        V((8 * rows, e), bf16),
        V((e, 8 * rows), bf16),
        V((8 * rows, 16 * rows), f32),
        V((8 * rows, 16 * rows), bf16),
        V((2 * rows, e), f32),
        V((2 * rows, e), f32),
        V((2 * rows, 1), f32),
        V((2 * rows, 1), f32),
        V((e, 2 * rows), bf16),
        V((8, rows), f32),
        V((8, rows), f32),
        V((8, 16 * rows), f32),
        V((8, 8, rows), f32),
        V((8 * rows, rows), f32),
        V((3, 1, 16 * rows), f32),
        V((3, 1, 16 * rows), f32),
        V((1, 16 * rows), f32),
        V((16, 1, 16 * rows), f32),
        V((1, 16 * rows), f32),
        V((1, 16 * rows), f32),
        V((2, 8, e, rows), bf16),
        V((8, e, rows), bf16),
        V((8, e, rows), bf16),
        V((2, 2, e // 2, rows), bf16),
        V((2, 2, e, rows), bf16),
        V((2, e, rows), bf16),
        V((8, rows, e), bf16),
        V((2, 2, half, e), bf16),
        V((2, 2, rows, e), bf16),
        V((2, rows, e), bf16),
        V((2 * rows, e), bf16),
        V((2, 2, 2, 4, 4, half, rows), bf16),
        V((2, 2, 4, 4, half, rows), bf16),
        V((2, 2, 4, 4, half, rows), bf16),
        V((3, 2, 4, half, rows), bf16),
        V((3, 2, 4, half, rows), bf16),
        V((2, 4, half, rows), bf16),
        V((2, 4, half, rows), bf16),
        V((3, 2, half, rows), bf16),
        V((3, 2, half, rows), bf16),
        V((2, 2, half, rows), bf16),
        V((3, half, rows), bf16),
        V((2, e), f32),
        V((16, 2, e), f32),
        V((8, 2, e), f32),
        pltpu.SemaphoreType.DMA((copies,)),
        pltpu.SemaphoreType.DMA((copies,)),
        pltpu.SemaphoreType.DMA((9,)),
    ]
    shapes = (
        jax.ShapeDtypeStruct((rows, e), bf16),
        jax.ShapeDtypeStruct((rows, e), bf16),
        jax.ShapeDtypeStruct((half, rows), f32),
        jax.ShapeDtypeStruct((1, e), f32),
        jax.ShapeDtypeStruct((1, e), f32),
    )
    anywhere = pl.BlockSpec(memory_space=pl.ANY)
    results = pl.pallas_call(
        kernel,
        out_shape=shapes,
        in_specs=[anywhere] * 9,
        out_specs=(vmem,) * 5,
        scratch_shapes=scratch,
        compiler_params=pltpu.CompilerParams(
            collective_id=0, has_side_effects=True, vmem_limit_bytes=60 * 1024 * 1024
        ),
        cost_estimate=pl.CostEstimate(flops=16_000_000_000, bytes_accessed=5_000_000, transcendentals=2_100_000),
    )(
        q_hidden, d_hidden, positive.reshape(1, rows), query_part.reshape(1, rows), loss_weight.reshape(1, rows),
        doc_part.reshape(1, rows), norm_gain.reshape(1, e), norm_bias.reshape(1, e), proj,
    )
    dq, dd, d_proj, d_gain, d_bias = pl.pallas_call(
        hand_over,
        out_shape=shapes,
        in_specs=[vmem] * 5,
        out_specs=(vmem,) * 5,
        cost_estimate=pl.CostEstimate(flops=0, bytes_accessed=1_200_000, transcendentals=0),
    )(*results)
    return dq, dd, d_proj.T, d_gain.reshape(e), d_bias.reshape(e)


def solution(mesh):
    placed = (
        P(("pb", "dev"), None),
        P(("dev", "pb"), None),
        P(("pb", "dev")),
        P(("pb", "dev")),
        P(("dev", "pb")),
        P(("pb", "dev")),
        P(),
        P(),
        P(),
    )
    return jax.shard_map(
        per_device,
        mesh=mesh,
        in_specs=placed,
        out_specs=(P(("pb", "dev"), None), P(("dev", "pb"), None), P("pb", "dev"), P(), P()),
        check_vma=False,
    )
```

```python
import jax
import jax.numpy as jnp
from jax import lax
from jax.experimental import pallas as pl
from jax.experimental.pallas import tpu as pltpu
from jax.sharding import PartitionSpec as P

logit_scale = 100.0
f32, bf16 = jnp.float32, jnp.bfloat16
MESH = pl.DeviceIdType.MESH
rows, width = 128, 1024
half, quarter = rows // 2, rows // 4
copies = 200
OFFSETS = ((0, 0), (1, 0), (0, 1), (0, 3), (0, 2), (1, 2), (1, 1), (1, 3))
NT = (((1,), (1,)), ((), ()))


def kernel(
    qh_hbm, dh_hbm, pos_hbm, qpart_hbm, weight_hbm, dpart_hbm, gain_hbm, bias_hbm, proj_hbm,
    dq, dd, dproj, dgain, dbias,
    qh, dh, pos_in, qpart_in, weight_in, dpart_in, gain, bias,
    proj, qbuf, dbuf, dt, st, gt, unit, normed, recip, inv, out_t, lab_q, lab_d, labs, dlab, dcol, mst, sst, lsend, lbuf,
    lsef, lrel, gqp, cbuf, sbuf, qfold, qring, qx, gdp, dfold, dring, dx_buf,
    ge, gs, hs0, hs1, r0, r1, h0, h1, f0, f1, gb, gba, gbb,
    send_sem, recv_sem, local_sem,
):
    pb, dev = lax.axis_index("pb"), lax.axis_index("dev")
    z, xl = pb // 2, lax.rem(pb, 2)
    y, xh, core = dev // 4, lax.rem(dev // 2, 2), lax.rem(dev, 2)

    def q_peer(dx, dy, dc=0):
        return (z * 2 + lax.rem(xl + dx, 2), lax.rem(y + dy, 4) * 4 + xh * 2 + lax.rem(core + dc, 2))

    def d_peer(dx, dz):
        return (lax.rem(z + dz, 4) * 2 + lax.rem(xl + dx, 2), y * 4 + lax.rem(xh + dx, 2) * 2 + core)

    started = []

    def send(src, dst, peer):
        n = len(started)
        copy = pltpu.make_async_remote_copy(
            src_ref=src, dst_ref=dst, send_sem=send_sem.at[n], recv_sem=recv_sem.at[n],
            device_id=peer, device_id_type=MESH,
        )
        copy.start()
        started.append(copy)
        return copy

    def arrive(*copies):
        for copy in copies:
            copy.wait_recv()

    q_offsets = [(dx, dy, dc) for dx in range(2) for dy in range(4) for dc in range(2)]
    d_offsets = [(dx, dz) for dx in range(2) for dz in range(4)]

    loads = []
    for n, (src, dst) in enumerate((
        (qh_hbm, qh), (dh_hbm, dh), (proj_hbm, proj), (gain_hbm, gain), (bias_hbm, bias),
        (pos_hbm, pos_in), (qpart_hbm, qpart_in), (weight_hbm, weight_in), (dpart_hbm, dpart_in),
    )):
        loads.append(pltpu.make_async_copy(src, dst, local_sem.at[n]))
        loads[-1].start()
    barrier = pltpu.get_barrier_semaphore()
    peers = [q_peer(*o) for o in q_offsets[1:]] + [d_peer(*o) for o in d_offsets[1:]]
    for peer in peers:
        pl.semaphore_signal(barrier, inc=1, device_id=peer, device_id_type=MESH)

    for n in (0, 1, 3, 4, 5, 6, 7, 8):
        loads[n].wait()
    lab_q[...] = jnp.zeros((8, rows), f32)
    lab_q[0:1, :] = pos_in[...].astype(f32)
    lab_q[1:2, :] = qpart_in[...].astype(f32)
    lab_q[2:3, :] = weight_in[...].astype(f32)
    lab_d[...] = jnp.broadcast_to(dpart_in[...].astype(f32), (8, rows))
    values = jnp.concatenate([qh[...], dh[...]], axis=0).astype(f32)
    centred = values - jnp.mean(values, axis=1, keepdims=True)
    r = lax.rsqrt(jnp.mean(centred * centred, axis=1, keepdims=True) + 1e-05)
    norm = centred * r
    recip[...] = r
    normed[...] = norm
    normal_out = (norm * gain[...] + bias[...]).astype(bf16)
    loads[2].wait()
    pl.semaphore_wait(barrier, len(peers))

    block = 8 * rows

    def q_at(core_index, k, offset=0):
        return pl.multiple_of(core_index * block + k * rows + offset, quarter)

    lab_copies = []
    for dx, dy, dc in q_offsets[1:]:
        k = OFFSETS.index((dx, (4 - dy) % 4))
        dst = labs.at[:, pl.ds(pl.multiple_of(core * block + k * rows, rows), rows)]
        lab_copies.append(send(lab_q, dst, q_peer(dx, dy, dc)))
    for dx, dz in d_offsets[1:]:
        lab_copies.append(send(lab_d, dlab.at[OFFSETS.index((dx, (4 - dz) % 4))], d_peer(dx, dz)))
    labs[:, pl.ds(pl.multiple_of(core * block, rows), rows)] = lab_q[...]
    dlab[0] = lab_d[...]

    embed = jnp.dot(normal_out, proj[...], preferred_element_type=f32)
    i = lax.rsqrt(jnp.sum(embed * embed, axis=1, keepdims=True) + 1e-06)
    inv[...] = i
    u = embed * i
    unit[...] = u
    qbuf[pl.ds(q_at(core, 0), rows), :] = u[:rows].astype(bf16)
    dbuf[0:rows, :] = u[rows:].astype(bf16)

    def q_part(k, first, count):
        return qbuf.at[pl.ds(q_at(core, k, first * quarter), count * quarter), :]

    def d_part(k, first, count):
        return dbuf.at[pl.ds(k * rows + first * quarter, count * quarter), :]

    def to_sibling(k):
        part = qbuf.at[pl.ds(pl.multiple_of(core * block + k * rows, rows), rows), :]
        return send(part, part, q_peer(0, 0, 1))

    q_got, d_got, sib = {}, {}, {}

    def hop(part, got, peer, k, span, to, way):
        got[to, span] = send(part(k, *span), part(to, *span), peer(1, 0) if way == 0 else peer(0, way))

    towers = ((q_part, q_got, q_peer), (d_part, d_got, d_peer))
    A, B, A0, A1, B0, B1 = (0, 2), (2, 2), (0, 1), (1, 1), (2, 1), (3, 1)
    for spans in (((A, 3, 1), (B, 2, 3), (A0, 1, 0), (B0, 1, 0)), ((B, 3, 1), (A, 2, 3), (A1, 1, 0), (B1, 1, 0))):
        for tower in towers:
            for span, to, way in spans:
                hop(*tower, 0, span, to, way)
    sib[0] = to_sibling(0)
    out_t[:, 0 : 2 * rows] = normal_out.T
    out_sib = send(out_t.at[:, pl.ds(0, 2 * rows)], out_t.at[:, pl.ds(2 * rows, 2 * rows)], q_peer(0, 0, 1))
    for tower in towers:
        arrive(tower[1][1, A0])
        hop(*tower, 1, A0, 7, 1)
    for tower in towers:
        arrive(tower[1][3, A])
        hop(*tower, 3, A, 4, 1)
        arrive(tower[1][2, B])
        hop(*tower, 2, B, 4, 3)
    for tower in towers:
        arrive(tower[1][1, B0])
        hop(*tower, 1, B0, 6, 3)
        arrive(tower[1][1, A1])
        hop(*tower, 1, A1, 7, 1)
        arrive(tower[1][1, B1])
        hop(*tower, 1, B1, 6, 3)
    for tower in towers:
        arrive(tower[1][3, B])
        hop(*tower, 3, B, 7, 0)
        arrive(tower[1][2, A])
        hop(*tower, 2, A, 6, 0)
    sib[1] = to_sibling(1)
    sib[2], sib[3] = to_sibling(2), to_sibling(3)
    arrive(*lab_copies)

    for k in range(8):
        dcol[k * rows : (k + 1) * rows, :] = jnp.broadcast_to(dlab[k, 0:1, :], (rows, rows)).T

    def transpose_docs(first, count):
        for k in range(first, first + count):
            dt[:, k * rows : (k + 1) * rows] = dbuf[k * rows : (k + 1) * rows, :].T

    lane = lax.broadcasted_iota(jnp.int32, (rows, 2 * rows), 0).astype(f32)

    def bases(k):
        to_pb, to_dev = d_peer(*OFFSETS[k])
        return ((to_dev * 8 + to_pb) * rows).astype(f32)

    def pair_cols(core_index, m):
        return pl.ds(pl.multiple_of(core_index * block + m * 2 * rows, 2 * rows), 2 * rows)

    def score(first, count, piece, cols):
        s = logit_scale * lax.dot_general(
            dbuf[first * rows : (first + count) * rows, :], qbuf[cols, :], NT, preferred_element_type=f32
        )
        pos, part = labs[0:1, cols], labs[1:2, cols]
        masked = []
        for n in range(count):
            k = first + n
            col = dcol[k * rows : (k + 1) * rows, :]
            valid = jnp.logical_or(part != jnp.concatenate([col, col], axis=1), lane == pos - bases(k))
            masked.append(jnp.where(valid, s[n * rows : (n + 1) * rows], jnp.float32(-1e30)))
        top = jnp.full((1, 2 * rows), -1e4, f32)
        for m in masked:
            top = jnp.maximum(top, jnp.max(m, axis=0, keepdims=True))
        total = jnp.zeros((1, 2 * rows), f32)
        for n, m in enumerate(masked):
            p = jnp.exp(m - top)
            total = total + jnp.sum(p, axis=0, keepdims=True)
            st[(first + n) * rows : (first + n + 1) * rows, cols] = p
        mst[piece, :, cols] = top
        sst[piece, :, cols] = total

    pieces = ((0, 4), (4, 2), (6, 2))

    def scores(piece, pairs):
        low, step, count = pairs

        def body(n, carry):
            m, c = low + step * (n // 2), lax.rem(n, 2)
            score(*pieces[piece], piece, pair_cols(c, m))
            return carry

        lax.fori_loop(0, 2 * count, body, 0)

    transpose_docs(0, 4)
    arrive(sib[0], sib[1], sib[2], sib[3])
    scores(0, (0, 1, 2))

    for a, b in ((A0, B0), (A1, B1)):
        for tower in towers:
            arrive(tower[1][7, a])
            hop(*tower, 7, a, 5, 1)
            arrive(tower[1][6, b])
            hop(*tower, 6, b, 5, 3)
    arrive(q_got[4, A], q_got[4, B])
    sib[4] = to_sibling(4)
    arrive(q_got[7, B], q_got[6, A])
    sib[6], sib[7] = to_sibling(6), to_sibling(7)
    arrive(d_got[7, B], d_got[6, A], d_got[4, A], d_got[4, B])
    transpose_docs(6, 2)
    transpose_docs(4, 1)
    scores(2, (0, 1, 2))
    arrive(sib[6], sib[7])
    scores(0, (3, 1, 1))
    scores(2, (3, 1, 1))

    arrive(*(q_got[5, span] for span in (A0, B0, A1, B1)))
    sib[5] = to_sibling(5)
    arrive(*(d_got[5, span] for span in (A0, B0, A1, B1)))
    transpose_docs(5, 1)
    scores(1, (0, 1, 2))
    scores(1, (3, 1, 1))
    arrive(sib[4], sib[5])
    scores(0, (2, 1, 1))
    scores(1, (2, 1, 1))
    scores(2, (2, 1, 1))

    top = jnp.maximum(jnp.maximum(mst[0], mst[1]), mst[2])
    total = sum(sst[b] * jnp.exp(mst[b] - top) for b in range(3))
    local = top + jnp.log(jnp.maximum(total, 1e-37))
    places = []
    for n in range(16):
        c, (dx, dy) = n // 8, OFFSETS[n % 8]
        places.append(c * 8 + lax.rem(y + dy, 4) * 2 + lax.rem(xl + dx, 2))
        lsend[pl.ds(places[-1], 1), :] = local[:, n * rows : (n + 1) * rows]
    lse_copies = [send(lsend, lbuf.at[s], q_peer(*q_offsets[s])) for s in range(1, 16)]
    lbuf[0] = lsend[...]
    arrive(*lse_copies)
    every = lbuf[...]
    top = jnp.max(every, axis=0)
    lsef[...] = top + jnp.log(jnp.sum(jnp.exp(every - top[None]), axis=0))
    for n, place in enumerate(places):
        lrel[:, n * rows : (n + 1) * rows] = lsef[pl.ds(place, 1), :]
    for b in range(3):
        sst[b] = jnp.exp(mst[b] - lrel[...])

    def grads(g, carry):
        cols = pl.ds(pl.multiple_of(g * 2 * rows, 2 * rows), 2 * rows)
        pos, weight = labs[0:1, cols], labs[2:3, cols]
        for k in range(8):
            scale = sst[0 if k < 4 else 1 if k < 6 else 2, :, cols]
            hit = jnp.where(lane == pos - bases(k), jnp.float32(1), jnp.float32(0))
            prob = st[k * rows : (k + 1) * rows, cols] * scale
            gt[k * rows : (k + 1) * rows, cols] = (weight * (prob - hit)).astype(bf16)
        return carry

    lax.fori_loop(0, 8, grads, 0)

    def doc_terms(m):
        def body(j, carry):
            cols = pl.ds(pl.multiple_of(j * 256, 256), 256)
            v = jnp.dot(
                gt[2 * m * rows : 2 * (m + 1) * rows, :], qbuf[:, cols], preferred_element_type=f32
            ).astype(bf16)
            gdp[2 * m, :, cols] = v[:rows]
            gdp[2 * m + 1, :, cols] = v[rows:]
            return carry

        lax.fori_loop(0, 4, body, 0)

    cores = {}

    def query_terms(m, other):
        cols = pair_cols(1 - core if other else core, m)

        def body(j, carry):
            part = pl.ds(pl.multiple_of(j * 512, 512), 512)
            v = jnp.dot(dt[part, :], gt[:, cols], preferred_element_type=f32).astype(bf16)
            gqp[other, 2 * m, part, :] = v[:, :rows]
            gqp[other, 2 * m + 1, part, :] = v[:, rows:]
            return carry

        lax.fori_loop(0, 2, body, 0)
        if other:
            span = pl.ds(2 * m, 2)
            cores[m] = send(gqp.at[1, span], cbuf.at[span], q_peer(0, 0, 1))

    def both_cores(k):
        if k // 2 in cores:
            arrive(cores.pop(k // 2))
        sbuf[k] = (gqp[0, k].astype(f32) + cbuf[k].astype(f32)).astype(bf16)

    slots = ((0, 2, 3, 4), (1, 6, 7, 5))

    def part_of(h, c, size):
        return pl.ds((2 * c + h) * size, size)

    def far_terms(src, fold, ring, peer, size, dx):
        far = slots[dx][3]
        return [
            [send(src.at[far, part_of(h, c, size), :], fold.at[dx, h, c], peer(0, 3 if h else 1)) for h in range(2)]
            for c in range(2)
        ]

    def near_terms(src, fold, ring, peer, size, dx):
        got = []
        for c in range(2):
            for h, way in ((1, 1), (0, 3)):
                part = part_of(h, c, size)
                got.append(send(src.at[slots[dx][1 if h else 2], part, :], ring.at[dx, 1 - h, part, :], peer(0, way)))
        return got

    def merged(src, fold, ring, peer, size, dx, c, waits):
        got = []
        for h in range(2):
            k, part = slots[dx][1 + h], part_of(h, c, size)
            rows_of = slice((2 * c + h) * size, (2 * c + h + 1) * size)
            arrive(waits[c][h])
            src[k, rows_of, :] = (src[k, rows_of, :].astype(f32) + fold[dx, h, c].astype(f32)).astype(bf16)
            got.append(send(src.at[k, part, :], ring.at[dx, h, part, :], peer(0, 3 if h else 1)))
        return got

    def ring_sum(src, ring, dx, low, size):
        span = slice(low, low + size)
        return src[dx, span, :].astype(f32) + ring[dx, 0, span, :].astype(f32) + ring[dx, 1, span, :].astype(f32)

    def across(src, ring, buf, peer, size, c):
        span = pl.ds(c * 2 * size, 2 * size)
        buf[0, c * 2 * size : (c + 1) * 2 * size, :] = ring_sum(src, ring, 1, c * 2 * size, 2 * size).astype(bf16)
        return send(buf.at[0, span, :], buf.at[1, span, :], peer(1, 0))

    D = (gdp, dfold, dring, d_peer, quarter)
    Q = (sbuf, qfold, qring, q_peer, width // 4)
    query_terms(2, 1)
    query_terms(2, 0)
    query_terms(3, 1)
    doc_terms(2)
    d_fold1 = far_terms(*D, 1)
    both_cores(5)
    q_fold1 = far_terms(*Q, 1)
    query_terms(3, 0)
    both_cores(6)
    both_cores(7)
    q_near1 = near_terms(*Q, 1)
    doc_terms(3)
    d_near1 = near_terms(*D, 1)
    both_cores(4)
    query_terms(1, 1)
    query_terms(0, 1)
    query_terms(1, 0)
    d_ring1 = [merged(*D, 1, 0, d_fold1)]
    q_ring1 = [merged(*Q, 1, 0, q_fold1)]
    d_ring1.append(merged(*D, 1, 1, d_fold1))
    q_ring1.append(merged(*Q, 1, 1, q_fold1))
    d_fold0 = far_terms(*D, 0)
    q_fold0 = far_terms(*Q, 0)
    doc_terms(1)
    d_near0 = near_terms(*D, 0)
    both_cores(2)
    both_cores(3)
    q_near0 = near_terms(*Q, 0)
    doc_terms(0)
    query_terms(0, 0)
    both_cores(1)
    both_cores(0)
    d_across, q_across = [], []
    arrive(*d_near1, *q_near1)
    for c in range(2):
        arrive(*d_ring1[c])
        d_across.append(across(gdp, dring, dx_buf, d_peer, quarter, c))
        arrive(*q_ring1[c])
        q_across.append(across(sbuf, qring, qx, q_peer, width // 4, c))
    d_ring0, q_ring0 = [], []
    for c in range(2):
        d_ring0 += merged(*D, 0, c, d_fold0)
        q_ring0 += merged(*Q, 0, c, q_fold0)

    left = lax.broadcasted_iota(jnp.int32, (rows, rows), 1) < half
    ge_copies = []

    def backward(g_unit, low, out):
        span = slice(low, low + rows)
        uu, nn = unit[span, :], normed[span, :]
        g = (g_unit - uu * jnp.sum(uu * g_unit, axis=1, keepdims=True)) * inv[span, :]
        for j in range(4):
            b0, b1 = g[:, 2 * j * rows : (2 * j + 1) * rows], g[:, (2 * j + 1) * rows : (2 * j + 2) * rows]
            n0 = jnp.where(left, b0, pltpu.roll(b1, half, 1))
            n1 = jnp.where(left, pltpu.roll(b0, half, 1), b1)
            ge[span, j * rows : (j + 1) * rows] = jnp.where(core == 0, n0, n1).astype(bf16)
            gs[span, j * rows : (j + 1) * rows] = jnp.where(core == 0, n1, n0).astype(bf16)
        ge_copies.append(send(gs.at[pl.ds(low, rows), :], ge.at[pl.ds(2 * rows + low, rows), :], q_peer(0, 0, 1)))
        g = g.astype(bf16)
        gn = lax.dot_general(g, proj[...], NT, preferred_element_type=f32)
        scaled = gn * gain[...]
        out[...] = (
            recip[span, :]
            * (scaled - jnp.mean(scaled, axis=1, keepdims=True) - nn * jnp.mean(scaled * nn, axis=1, keepdims=True))
        ).astype(bf16)
        return jnp.sum(gn * nn, axis=0, keepdims=True), jnp.sum(gn, axis=0, keepdims=True)

    arrive(*d_near0, *d_ring0, *d_across)
    g_doc = logit_scale * (ring_sum(gdp, dring, 0, 0, rows) + dx_buf[1].astype(f32))
    gain_d, bias_d = backward(g_doc, rows, dd)
    arrive(*q_near0, *q_ring0, *q_across)
    gain_q, bias_q = backward(logit_scale * (ring_sum(sbuf, qring, 0, 0, width) + qx[1].astype(f32)).T, 0, dq)

    gb[0:1, :] = gain_d + gain_q
    gb[1:2, :] = bias_d + bias_q
    order = (y * 2 + xl) * 2 + core
    gb_copies = [send(gb, gba.at[order], q_peer(*o)) for o in q_offsets[1:]]
    gba[order] = gb[...]

    low_left = left[:half]
    arrive(out_sib, *ge_copies)

    def head(n, carry):
        for a in range(2):
            v = jnp.dot(
                out_t[pl.ds(pl.multiple_of((2 * n + a) * rows, rows), rows), :], ge[...], preferred_element_type=f32
            )
            for j in range(4):
                upper, lower = v[:half, j * rows : (j + 1) * rows], v[half:, j * rows : (j + 1) * rows]
                for b in range(2):
                    if b == 0:
                        w = jnp.where(low_left, upper, pltpu.roll(lower, half, 1)).astype(bf16)
                    else:
                        w = jnp.where(low_left, pltpu.roll(upper, half, 1), lower).astype(bf16)
                    hs0[b, n, a, j] = w[:quarter]
                    hs1[(a + b) % 2, j, b, n] = w[quarter:]
        return carry

    lax.fori_loop(0, 4, head, 0)
    diagonal = lax.rem(xl + xh, 2)
    first0, first1 = [], []
    for s, (dx, dz) in enumerate(d_offsets[1:]):
        first0.append(send(hs0.at[lax.rem(xh + dx, 2), lax.rem(z + dz, 4)], r0.at[s], d_peer(dx, dz)))
        dy = dz
        first1.append(send(hs1.at[lax.rem(diagonal + dx, 2), lax.rem(y + dy, 4)], r1.at[s], q_peer(dx, dy)))

    arrive(*gb_copies)
    acc = gba[0]
    for n in range(1, 16):
        acc = acc + gba[n]
    order = z * 2 + xh
    gbb[order] = acc
    gb_copies = [send(gbb.at[order], gbb.at[order], d_peer(*o)) for o in d_offsets[1:]]

    def total_of(own, got):
        return own.astype(f32) + sum(got[n].astype(f32) for n in range(7))

    arrive(*first0)
    h0[...] = total_of(hs0[xh, z], r0).astype(bf16)
    second0 = [
        send(h0.at[lax.rem(xl + dx, 2), lax.rem(y + dy, 4)], f0.at[s], q_peer(dx, dy))
        for s, (dx, dy) in enumerate(d_offsets[1:])
    ]
    arrive(*first1)
    h1[...] = total_of(hs1[diagonal, y], r1).astype(bf16)
    second1 = [
        send(h1.at[lax.rem(xh + dx, 2), lax.rem(z + dz, 4)], f1.at[s], d_peer(dx, dz))
        for s, (dx, dz) in enumerate(d_offsets[1:])
    ]
    arrive(*second0, *second1)
    final = jnp.concatenate([total_of(h0[xl, y], f0), total_of(h1[xh, z], f1)], axis=0)
    dproj[:, 0:half] = final[:, :half].T
    dproj[:, half:rows] = final[:, half:].T

    arrive(*gb_copies)
    acc = gbb[0]
    for n in range(1, 8):
        acc = acc + gbb[n]
    dgain[...] = acc[0:1]
    dbias[...] = acc[1:2]

    for copy in started:
        copy.wait_send()


def hand_over(*refs):
    for src, dst in zip(refs[:5], refs[5:]):
        dst[...] = src[...]


def per_device(
    q_hidden, d_hidden, positive, query_part, doc_part, loss_weight, norm_gain, norm_bias, proj
):
    vmem = pl.BlockSpec(memory_space=pltpu.VMEM)
    V = pltpu.VMEM
    e = width
    scratch = [
        V((rows, e), bf16),
        V((rows, e), bf16),
        V((1, rows), jnp.int32),
        V((1, rows), jnp.int32),
        V((1, rows), bf16),
        V((1, rows), jnp.int32),
        V((1, e), f32),
        V((1, e), f32),
        V((e, e), bf16),
        V((16 * rows, e), bf16),
        V((8 * rows, e), bf16),
        V((e, 8 * rows), bf16),
        V((8 * rows, 16 * rows), f32),
        V((8 * rows, 16 * rows), bf16),
        V((2 * rows, e), f32),
        V((2 * rows, e), f32),
        V((2 * rows, 1), f32),
        V((2 * rows, 1), f32),
        V((e, 4 * rows), bf16),
        V((8, rows), f32),
        V((8, rows), f32),
        V((8, 16 * rows), f32),
        V((8, 8, rows), f32),
        V((8 * rows, rows), f32),
        V((3, 1, 16 * rows), f32),
        V((3, 1, 16 * rows), f32),
        V((16, rows), f32),
        V((16, 16, rows), f32),
        V((16, rows), f32),
        V((1, 16 * rows), f32),
        V((2, 8, e, rows), bf16),
        V((8, e, rows), bf16),
        V((8, e, rows), bf16),
        V((2, 2, 2, e // 4, rows), bf16),
        V((2, 2, e, rows), bf16),
        V((2, e, rows), bf16),
        V((8, rows, e), bf16),
        V((2, 2, 2, quarter, e), bf16),
        V((2, 2, rows, e), bf16),
        V((2, rows, e), bf16),
        V((4 * rows, 4 * rows), bf16),
        V((2 * rows, 4 * rows), bf16),
        V((2, 4, 2, 4, quarter, rows), bf16),
        V((2, 4, 2, 4, quarter, rows), bf16),
        V((7, 2, 4, quarter, rows), bf16),
        V((7, 2, 4, quarter, rows), bf16),
        V((2, 4, quarter, rows), bf16),
        V((2, 4, quarter, rows), bf16),
        V((7, quarter, rows), bf16),
        V((7, quarter, rows), bf16),
        V((2, e), f32),
        V((16, 2, e), f32),
        V((8, 2, e), f32),
        pltpu.SemaphoreType.DMA((copies,)),
        pltpu.SemaphoreType.DMA((copies,)),
        pltpu.SemaphoreType.DMA((9,)),
    ]
    shapes = (
        jax.ShapeDtypeStruct((rows, e), bf16),
        jax.ShapeDtypeStruct((rows, e), bf16),
        jax.ShapeDtypeStruct((half, rows), f32),
        jax.ShapeDtypeStruct((1, e), f32),
        jax.ShapeDtypeStruct((1, e), f32),
    )
    anywhere = pl.BlockSpec(memory_space=pl.ANY)
    results = pl.pallas_call(
        kernel,
        out_shape=shapes,
        in_specs=[anywhere] * 9,
        out_specs=(vmem,) * 5,
        scratch_shapes=scratch,
        compiler_params=pltpu.CompilerParams(
            collective_id=0, has_side_effects=True, vmem_limit_bytes=60 * 1024 * 1024
        ),
        cost_estimate=pl.CostEstimate(flops=16_000_000_000, bytes_accessed=5_000_000, transcendentals=2_100_000),
    )(
        q_hidden, d_hidden, positive.reshape(1, rows), query_part.reshape(1, rows), loss_weight.reshape(1, rows),
        doc_part.reshape(1, rows), norm_gain.reshape(1, e), norm_bias.reshape(1, e), proj,
    )
    dq, dd, d_proj, d_gain, d_bias = pl.pallas_call(
        hand_over,
        out_shape=shapes,
        in_specs=[vmem] * 5,
        out_specs=(vmem,) * 5,
        cost_estimate=pl.CostEstimate(flops=0, bytes_accessed=1_200_000, transcendentals=0),
    )(*results)
    return dq, dd, d_proj.T, d_gain.reshape(e), d_bias.reshape(e)


def solution(mesh):
    placed = (
        P(("pb", "dev"), None),
        P(("dev", "pb"), None),
        P(("pb", "dev")),
        P(("pb", "dev")),
        P(("dev", "pb")),
        P(("pb", "dev")),
        P(),
        P(),
        P(),
    )
    return jax.shard_map(
        per_device,
        mesh=mesh,
        in_specs=placed,
        out_specs=(P(("pb", "dev"), None), P(("dev", "pb"), None), P("pb", "dev"), P(), P()),
        check_vma=False,
    )
```

```python
import jax
import jax.numpy as jnp
from jax import lax
from jax.experimental import pallas as pl
from jax.experimental.pallas import tpu as pltpu
from jax.sharding import PartitionSpec as P

logit_scale = 100.0
f32, bf16 = jnp.float32, jnp.bfloat16
MESH = pl.DeviceIdType.MESH
rows, width = 128, 1024
half, quarter = rows // 2, rows // 4
copies = 200
OFFSETS = ((0, 0), (1, 0), (0, 1), (0, 3), (0, 2), (1, 2), (1, 1), (1, 3))
NT = (((1,), (1,)), ((), ()))


def kernel(
    qh_hbm, dh_hbm, pos_hbm, qpart_hbm, weight_hbm, dpart_hbm, gain_hbm, bias_hbm, proj_hbm,
    dq, dd, dproj, dgain, dbias,
    qh, dh, pos_in, qpart_in, weight_in, dpart_in, gain, bias,
    proj, qbuf, dbuf, dt, st, gt, unit, normed, recip, inv, out_t, lab_q, lab_d, labs, dlab, dcol, mst, sst, lsend, lbuf,
    lsef, lrel, gqp, cbuf, sbuf, qfold, qring, qx, gdp, dfold, dring, dx_buf,
    ge, gs, gns, hs0, hs1, r0, r1, h0, h1, f0, f1, gb, gba, gbb,
    send_sem, recv_sem, local_sem,
):
    pb, dev = lax.axis_index("pb"), lax.axis_index("dev")
    z, xl = pb // 2, lax.rem(pb, 2)
    y, xh, core = dev // 4, lax.rem(dev // 2, 2), lax.rem(dev, 2)

    def q_peer(dx, dy, dc=0):
        return (z * 2 + lax.rem(xl + dx, 2), lax.rem(y + dy, 4) * 4 + xh * 2 + lax.rem(core + dc, 2))

    def d_peer(dx, dz):
        return (lax.rem(z + dz, 4) * 2 + lax.rem(xl + dx, 2), y * 4 + lax.rem(xh + dx, 2) * 2 + core)

    started = []

    def send(src, dst, peer):
        n = len(started)
        copy = pltpu.make_async_remote_copy(
            src_ref=src, dst_ref=dst, send_sem=send_sem.at[n], recv_sem=recv_sem.at[n],
            device_id=peer, device_id_type=MESH,
        )
        copy.start()
        started.append(copy)
        return copy

    def arrive(*copies):
        for copy in copies:
            copy.wait_recv()

    q_offsets = [(dx, dy, dc) for dx in range(2) for dy in range(4) for dc in range(2)]
    d_offsets = [(dx, dz) for dx in range(2) for dz in range(4)]

    loads = []
    for n, (src, dst) in enumerate((
        (qh_hbm, qh), (dh_hbm, dh), (proj_hbm, proj), (gain_hbm, gain), (bias_hbm, bias),
        (pos_hbm, pos_in), (qpart_hbm, qpart_in), (weight_hbm, weight_in), (dpart_hbm, dpart_in),
    )):
        loads.append(pltpu.make_async_copy(src, dst, local_sem.at[n]))
        loads[-1].start()
    barrier = pltpu.get_barrier_semaphore()
    peers = [q_peer(*o) for o in q_offsets[1:]] + [d_peer(*o) for o in d_offsets[1:]]
    for peer in peers:
        pl.semaphore_signal(barrier, inc=1, device_id=peer, device_id_type=MESH)

    for n in (0, 1, 3, 4, 5, 6, 7, 8):
        loads[n].wait()
    lab_q[...] = jnp.zeros((8, rows), f32)
    lab_q[0:1, :] = pos_in[...].astype(f32)
    lab_q[1:2, :] = qpart_in[...].astype(f32)
    lab_q[2:3, :] = weight_in[...].astype(f32)
    lab_d[...] = jnp.broadcast_to(dpart_in[...].astype(f32), (8, rows))
    values = jnp.concatenate([qh[...], dh[...]], axis=0).astype(f32)
    centred = values - jnp.mean(values, axis=1, keepdims=True)
    r = lax.rsqrt(jnp.mean(centred * centred, axis=1, keepdims=True) + 1e-05)
    norm = centred * r
    recip[...] = r
    normed[...] = norm
    normal_out = (norm * gain[...] + bias[...]).astype(bf16)
    loads[2].wait()
    pl.semaphore_wait(barrier, len(peers))

    block = 8 * rows

    def q_at(core_index, k, offset=0):
        return pl.multiple_of(core_index * block + k * rows + offset, quarter)

    embed = jnp.dot(normal_out, proj[...], preferred_element_type=f32)
    i = lax.rsqrt(jnp.sum(embed * embed, axis=1, keepdims=True) + 1e-06)
    inv[...] = i
    u = embed * i
    unit[...] = u
    qbuf[pl.ds(q_at(core, 0), rows), :] = u[:rows].astype(bf16)
    dbuf[0:rows, :] = u[rows:].astype(bf16)

    def q_part(k, first, count):
        return qbuf.at[pl.ds(q_at(core, k, first * quarter), count * quarter), :]

    def d_part(k, first, count):
        return dbuf.at[pl.ds(k * rows + first * quarter, count * quarter), :]

    def to_sibling(k):
        part = qbuf.at[pl.ds(pl.multiple_of(core * block + k * rows, rows), rows), :]
        return send(part, part, q_peer(0, 0, 1))

    q_got, d_got, sib = {}, {}, {}

    def hop(part, got, peer, k, span, to, way):
        got[to, span] = send(part(k, *span), part(to, *span), peer(1, 0) if way == 0 else peer(0, way))

    towers = ((q_part, q_got, q_peer), (d_part, d_got, d_peer))
    A, B, A0, A1, B0, B1 = (0, 2), (2, 2), (0, 1), (1, 1), (2, 1), (3, 1)
    for spans in (((A, 3, 1), (B, 2, 3), (A0, 1, 0), (B0, 1, 0)), ((B, 3, 1), (A, 2, 3), (A1, 1, 0), (B1, 1, 0))):
        for tower in towers:
            for span, to, way in spans:
                hop(*tower, 0, span, to, way)
    sib[0] = to_sibling(0)
    lab_copies = []
    for dx, dy, dc in q_offsets[1:]:
        k = OFFSETS.index((dx, (4 - dy) % 4))
        dst = labs.at[:, pl.ds(pl.multiple_of(core * block + k * rows, rows), rows)]
        lab_copies.append(send(lab_q, dst, q_peer(dx, dy, dc)))
    for dx, dz in d_offsets[1:]:
        lab_copies.append(send(lab_d, dlab.at[OFFSETS.index((dx, (4 - dz) % 4))], d_peer(dx, dz)))
    labs[:, pl.ds(pl.multiple_of(core * block, rows), rows)] = lab_q[...]
    dlab[0] = lab_d[...]
    out_t[:, 0 : 2 * rows] = normal_out.T
    out_sib = send(out_t.at[:, pl.ds(0, 2 * rows)], out_t.at[:, pl.ds(2 * rows, 2 * rows)], q_peer(0, 0, 1))
    for tower in towers:
        arrive(tower[1][1, A0])
        hop(*tower, 1, A0, 7, 1)
    for tower in towers:
        arrive(tower[1][3, A])
        hop(*tower, 3, A, 4, 1)
        arrive(tower[1][2, B])
        hop(*tower, 2, B, 4, 3)
    for tower in towers:
        arrive(tower[1][1, B0])
        hop(*tower, 1, B0, 6, 3)
        arrive(tower[1][1, A1])
        hop(*tower, 1, A1, 7, 1)
        arrive(tower[1][1, B1])
        hop(*tower, 1, B1, 6, 3)
    for tower in towers:
        arrive(tower[1][3, B])
        hop(*tower, 3, B, 7, 0)
        arrive(tower[1][2, A])
        hop(*tower, 2, A, 6, 0)
    sib[1] = to_sibling(1)
    sib[2], sib[3] = to_sibling(2), to_sibling(3)
    arrive(*lab_copies)

    for k in range(8):
        dcol[k * rows : (k + 1) * rows, :] = jnp.broadcast_to(dlab[k, 0:1, :], (rows, rows)).T

    def transpose_docs(first, count):
        for k in range(first, first + count):
            dt[:, k * rows : (k + 1) * rows] = dbuf[k * rows : (k + 1) * rows, :].T

    def lane(wide):
        return lax.broadcasted_iota(jnp.int32, (rows, wide), 0).astype(f32)

    def bases(k):
        to_pb, to_dev = d_peer(*OFFSETS[k])
        return ((to_dev * 8 + to_pb) * rows).astype(f32)

    def pair_cols(core_index, m, count=1):
        return pl.ds(pl.multiple_of(core_index * block + m * 2 * rows, 2 * rows), count * 2 * rows)

    def score(first, count, piece, cols):
        wide = cols.size
        s = logit_scale * lax.dot_general(
            dbuf[first * rows : (first + count) * rows, :], qbuf[cols, :], NT, preferred_element_type=f32
        )
        pos, part = labs[0:1, cols], labs[1:2, cols]
        masked = []
        for n in range(count):
            k = first + n
            col = jnp.concatenate([dcol[k * rows : (k + 1) * rows, :]] * (wide // rows), axis=1)
            valid = jnp.logical_or(part != col, lane(wide) == pos - bases(k))
            masked.append(jnp.where(valid, s[n * rows : (n + 1) * rows], jnp.float32(-1e30)))
        top = jnp.full((1, wide), -1e4, f32)
        for m in masked:
            top = jnp.maximum(top, jnp.max(m, axis=0, keepdims=True))
        total = jnp.zeros((1, wide), f32)
        for n, m in enumerate(masked):
            p = jnp.exp(m - top)
            total = total + jnp.sum(p, axis=0, keepdims=True)
            st[(first + n) * rows : (first + n + 1) * rows, cols] = p
        mst[piece, :, cols] = top
        sst[piece, :, cols] = total

    pieces = ((0, 4), (4, 2), (6, 2))

    def scores(piece, m, count):
        def body(c, carry):
            score(*pieces[piece], piece, pair_cols(c, m, count))
            return carry

        lax.fori_loop(0, 2, body, 0)

    transpose_docs(0, 4)
    arrive(sib[0], sib[1], sib[2], sib[3])
    scores(0, 0, 1)
    scores(0, 1, 1)

    for a, b in ((A0, B0), (A1, B1)):
        for tower in towers:
            arrive(tower[1][7, a])
            hop(*tower, 7, a, 5, 1)
            arrive(tower[1][6, b])
            hop(*tower, 6, b, 5, 3)
    arrive(q_got[4, A], q_got[4, B])
    sib[4] = to_sibling(4)
    arrive(q_got[7, B], q_got[6, A])
    sib[6], sib[7] = to_sibling(6), to_sibling(7)
    arrive(d_got[7, B], d_got[6, A], d_got[4, A], d_got[4, B])
    transpose_docs(6, 2)
    transpose_docs(4, 1)
    scores(2, 0, 2)
    arrive(sib[6], sib[7])
    scores(0, 3, 1)
    scores(2, 3, 1)

    arrive(*(q_got[5, span] for span in (A0, B0, A1, B1)))
    sib[5] = to_sibling(5)
    arrive(*(d_got[5, span] for span in (A0, B0, A1, B1)))
    transpose_docs(5, 1)
    scores(1, 0, 2)
    arrive(sib[4], sib[5])
    scores(1, 2, 2)
    scores(0, 2, 1)
    scores(2, 2, 1)

    top = jnp.maximum(jnp.maximum(mst[0], mst[1]), mst[2])
    total = sum(sst[b] * jnp.exp(mst[b] - top) for b in range(3))
    local = top + jnp.log(jnp.maximum(total, 1e-37))
    places = []
    for n in range(16):
        c, (dx, dy) = n // 8, OFFSETS[n % 8]
        places.append(c * 8 + lax.rem(y + dy, 4) * 2 + lax.rem(xl + dx, 2))
        lsend[pl.ds(places[-1], 1), :] = local[:, n * rows : (n + 1) * rows]
    lse_copies = [send(lsend, lbuf.at[s], q_peer(*q_offsets[s])) for s in range(1, 16)]
    lbuf[0] = lsend[...]
    arrive(*lse_copies)
    every = lbuf[...]
    top = jnp.max(every, axis=0)
    lsef[...] = top + jnp.log(jnp.sum(jnp.exp(every - top[None]), axis=0))
    for n, place in enumerate(places):
        lrel[:, n * rows : (n + 1) * rows] = lsef[pl.ds(place, 1), :]
    for b in range(3):
        sst[b] = jnp.exp(mst[b] - lrel[...])

    def grads(c, m, ks):
        cols = pair_cols(c, m)
        pos, weight = labs[0:1, cols], labs[2:3, cols]
        for k in ks:
            scale = sst[0 if k < 4 else 1 if k < 6 else 2, :, cols]
            hit = jnp.where(lane(2 * rows) == pos - bases(k), jnp.float32(1), jnp.float32(0))
            prob = st[k * rows : (k + 1) * rows, cols] * scale
            gt[k * rows : (k + 1) * rows, cols] = (weight * (prob - hit)).astype(bf16)

    def grads_of(ms, ks):
        def body(c, carry):
            for m in ms:
                grads(c, m, ks)
            return carry

        lax.fori_loop(0, 2, body, 0)


    def doc_terms(m):
        def body(j, carry):
            cols = pl.ds(pl.multiple_of(j * 512, 512), 512)
            v = jnp.dot(
                gt[2 * m * rows : 2 * (m + 1) * rows, :], qbuf[:, cols], preferred_element_type=f32
            ).astype(bf16)
            gdp[2 * m, :, cols] = v[:rows]
            gdp[2 * m + 1, :, cols] = v[rows:]
            return carry

        lax.fori_loop(0, 2, body, 0)

    cores = {}

    def query_terms(m, other):
        cols = pair_cols(1 - core if other else core, m)

        v = jnp.dot(dt[...], gt[:, cols], preferred_element_type=f32).astype(bf16)
        gqp[other, 2 * m] = v[:, :rows]
        gqp[other, 2 * m + 1] = v[:, rows:]
        if other:
            span = pl.ds(2 * m, 2)
            cores[m] = send(gqp.at[1, span], cbuf.at[span], q_peer(0, 0, 1))

    def both_cores(k):
        if k // 2 in cores:
            arrive(cores.pop(k // 2))
        sbuf[k] = (gqp[0, k].astype(f32) + cbuf[k].astype(f32)).astype(bf16)

    slots = ((0, 2, 3, 4), (1, 6, 7, 5))

    def part_of(h, c, size):
        return pl.ds((2 * c + h) * size, size)

    def far_terms(src, fold, ring, peer, size, dx):
        far = slots[dx][3]
        return [
            [send(src.at[far, part_of(h, c, size), :], fold.at[dx, h, c], peer(0, 3 if h else 1)) for h in range(2)]
            for c in range(2)
        ]

    def near_terms(src, fold, ring, peer, size, dx):
        got = []
        for c in range(2):
            for h, way in ((1, 1), (0, 3)):
                part = part_of(h, c, size)
                got.append(send(src.at[slots[dx][1 if h else 2], part, :], ring.at[dx, 1 - h, part, :], peer(0, way)))
        return got

    def merged(src, fold, ring, peer, size, dx, c, waits):
        got = []
        for h in range(2):
            k, part = slots[dx][1 + h], part_of(h, c, size)
            rows_of = slice((2 * c + h) * size, (2 * c + h + 1) * size)
            arrive(waits[c][h])
            src[k, rows_of, :] = (src[k, rows_of, :].astype(f32) + fold[dx, h, c].astype(f32)).astype(bf16)
            got.append(send(src.at[k, part, :], ring.at[dx, h, part, :], peer(0, 3 if h else 1)))
        return got

    def ring_sum(src, ring, dx, low, size):
        span = slice(low, low + size)
        return src[dx, span, :].astype(f32) + ring[dx, 0, span, :].astype(f32) + ring[dx, 1, span, :].astype(f32)

    def across(src, ring, buf, peer, size, c):
        span = pl.ds(c * 2 * size, 2 * size)
        buf[0, c * 2 * size : (c + 1) * 2 * size, :] = ring_sum(src, ring, 1, c * 2 * size, 2 * size).astype(bf16)
        return send(buf.at[0, span, :], buf.at[1, span, :], peer(1, 0))

    D = (gdp, dfold, dring, d_peer, quarter)
    Q = (sbuf, qfold, qring, q_peer, width // 4)
    grads_of((2,), range(8))
    query_terms(2, 1)
    query_terms(2, 0)
    grads_of((0, 1, 3), (4, 5))
    doc_terms(2)
    d_fold1 = far_terms(*D, 1)
    both_cores(5)
    q_fold1 = far_terms(*Q, 1)
    grads_of((3,), (0, 1, 2, 3, 6, 7))
    query_terms(3, 1)
    grads_of((0, 1), (6, 7))
    doc_terms(3)
    d_near1 = near_terms(*D, 1)
    query_terms(3, 0)
    both_cores(6)
    both_cores(7)
    q_near1 = near_terms(*Q, 1)
    both_cores(4)
    grads_of((0, 1), (0, 1, 2, 3))
    query_terms(1, 1)
    d_ring1 = [merged(*D, 1, 0, d_fold1)]
    q_ring1 = [merged(*Q, 1, 0, q_fold1)]
    d_ring1.append(merged(*D, 1, 1, d_fold1))
    q_ring1.append(merged(*Q, 1, 1, q_fold1))
    d_fold0 = far_terms(*D, 0)
    q_fold0 = far_terms(*Q, 0)
    query_terms(0, 1)
    doc_terms(1)
    d_near0 = near_terms(*D, 0)
    query_terms(1, 0)
    both_cores(2)
    both_cores(3)
    q_near0 = near_terms(*Q, 0)
    doc_terms(0)
    query_terms(0, 0)
    both_cores(1)
    both_cores(0)
    d_across, q_across = [], []
    arrive(*d_near1, *q_near1)
    for c in range(2):
        arrive(*d_ring1[c])
        d_across.append(across(gdp, dring, dx_buf, d_peer, quarter, c))
        arrive(*q_ring1[c])
        q_across.append(across(sbuf, qring, qx, q_peer, width // 4, c))
    d_ring0, q_ring0 = [], []
    for c in range(2):
        d_ring0 += merged(*D, 0, c, d_fold0)
        q_ring0 += merged(*Q, 0, c, q_fold0)

    left = lax.broadcasted_iota(jnp.int32, (2 * rows, rows), 1) < half
    arrive(*d_near0, *d_ring0, *d_across)
    g_doc = ring_sum(gdp, dring, 0, 0, rows) + dx_buf[1].astype(f32)
    arrive(*q_near0, *q_ring0, *q_across)
    g_query = (ring_sum(sbuf, qring, 0, 0, width) + qx[1].astype(f32)).T
    g_unit = logit_scale * jnp.concatenate([g_query, g_doc], axis=0)
    uu = unit[...]
    g = (g_unit - uu * jnp.sum(uu * g_unit, axis=1, keepdims=True)) * inv[...]
    for j in range(4):
        b0, b1 = g[:, 2 * j * rows : (2 * j + 1) * rows], g[:, (2 * j + 1) * rows : (2 * j + 2) * rows]
        n0 = jnp.where(left, b0, pltpu.roll(b1, half, 1))
        n1 = jnp.where(left, pltpu.roll(b0, half, 1), b1)
        ge[0 : 2 * rows, j * rows : (j + 1) * rows] = jnp.where(core == 0, n0, n1).astype(bf16)
        gs[:, j * rows : (j + 1) * rows] = jnp.where(core == 0, n1, n0).astype(bf16)
    ge_copy = send(gs, ge.at[pl.ds(2 * rows, 2 * rows), :], q_peer(0, 0, 1))
    gn = lax.dot_general(g.astype(bf16), proj[...], NT, preferred_element_type=f32)
    nn = normed[...]
    gns[...] = gn
    gb[0:1, :] = jnp.sum(gn * nn, axis=0, keepdims=True)
    gb[1:2, :] = jnp.sum(gn, axis=0, keepdims=True)
    order = (y * 2 + xl) * 2 + core
    gb_copies = [send(gb, gba.at[order], q_peer(*o)) for o in q_offsets[1:]]
    gba[order] = gb[...]

    low_left = left[:half]
    arrive(out_sib, ge_copy)

    def head(n, carry):
        for a in range(2):
            v = jnp.dot(
                out_t[pl.ds(pl.multiple_of((2 * n + a) * rows, rows), rows), :], ge[...], preferred_element_type=f32
            )
            for j in range(4):
                upper, lower = v[:half, j * rows : (j + 1) * rows], v[half:, j * rows : (j + 1) * rows]
                for b in range(2):
                    if b == 0:
                        w = jnp.where(low_left, upper, pltpu.roll(lower, half, 1)).astype(bf16)
                    else:
                        w = jnp.where(low_left, pltpu.roll(upper, half, 1), lower).astype(bf16)
                    hs0[b, n, a, j] = w[:quarter]
                    hs1[(a + b) % 2, j, b, n] = w[quarter:]
        return carry

    lax.fori_loop(0, 4, head, 0)
    diagonal = lax.rem(xl + xh, 2)
    first0, first1 = [], []
    for s, (dx, dz) in enumerate(d_offsets[1:]):
        first0.append(send(hs0.at[lax.rem(xh + dx, 2), lax.rem(z + dz, 4)], r0.at[s], d_peer(dx, dz)))
        dy = dz
        first1.append(send(hs1.at[lax.rem(diagonal + dx, 2), lax.rem(y + dy, 4)], r1.at[s], q_peer(dx, dy)))
    gn, nn = gns[...], normed[...]
    scaled = gn * gain[...]
    grad_h = recip[...] * (
        scaled - jnp.mean(scaled, axis=1, keepdims=True) - nn * jnp.mean(scaled * nn, axis=1, keepdims=True)
    )
    dq[...] = grad_h[:rows].astype(bf16)
    dd[...] = grad_h[rows:].astype(bf16)

    arrive(*gb_copies)
    acc = gba[0]
    for n in range(1, 16):
        acc = acc + gba[n]
    order = z * 2 + xh
    gbb[order] = acc
    gb_copies = [send(gbb.at[order], gbb.at[order], d_peer(*o)) for o in d_offsets[1:]]

    def total_of(own, got):
        return own.astype(f32) + sum(got[n].astype(f32) for n in range(7))

    arrive(*first0)
    h0[...] = total_of(hs0[xh, z], r0).astype(bf16)
    second0 = [
        send(h0.at[lax.rem(xl + dx, 2), lax.rem(y + dy, 4)], f0.at[s], q_peer(dx, dy))
        for s, (dx, dy) in enumerate(d_offsets[1:])
    ]
    arrive(*first1)
    h1[...] = total_of(hs1[diagonal, y], r1).astype(bf16)
    second1 = [
        send(h1.at[lax.rem(xh + dx, 2), lax.rem(z + dz, 4)], f1.at[s], d_peer(dx, dz))
        for s, (dx, dz) in enumerate(d_offsets[1:])
    ]
    arrive(*second0, *second1)
    final = jnp.concatenate([total_of(h0[xl, y], f0), total_of(h1[xh, z], f1)], axis=0)
    dproj[:, 0:half] = final[:, :half].T
    dproj[:, half:rows] = final[:, half:].T

    arrive(*gb_copies)
    acc = gbb[0]
    for n in range(1, 8):
        acc = acc + gbb[n]
    dgain[...] = acc[0:1]
    dbias[...] = acc[1:2]

    for copy in started:
        copy.wait_send()


def hand_over(*refs):
    for src, dst in zip(refs[:5], refs[5:]):
        dst[...] = src[...]


def per_device(
    q_hidden, d_hidden, positive, query_part, doc_part, loss_weight, norm_gain, norm_bias, proj
):
    vmem = pl.BlockSpec(memory_space=pltpu.VMEM)
    V = pltpu.VMEM
    e = width
    scratch = [
        V((rows, e), bf16),
        V((rows, e), bf16),
        V((1, rows), jnp.int32),
        V((1, rows), jnp.int32),
        V((1, rows), bf16),
        V((1, rows), jnp.int32),
        V((1, e), f32),
        V((1, e), f32),
        V((e, e), bf16),
        V((16 * rows, e), bf16),
        V((8 * rows, e), bf16),
        V((e, 8 * rows), bf16),
        V((8 * rows, 16 * rows), f32),
        V((8 * rows, 16 * rows), bf16),
        V((2 * rows, e), f32),
        V((2 * rows, e), f32),
        V((2 * rows, 1), f32),
        V((2 * rows, 1), f32),
        V((e, 4 * rows), bf16),
        V((8, rows), f32),
        V((8, rows), f32),
        V((8, 16 * rows), f32),
        V((8, 8, rows), f32),
        V((8 * rows, rows), f32),
        V((3, 1, 16 * rows), f32),
        V((3, 1, 16 * rows), f32),
        V((16, rows), f32),
        V((16, 16, rows), f32),
        V((16, rows), f32),
        V((1, 16 * rows), f32),
        V((2, 8, e, rows), bf16),
        V((8, e, rows), bf16),
        V((8, e, rows), bf16),
        V((2, 2, 2, e // 4, rows), bf16),
        V((2, 2, e, rows), bf16),
        V((2, e, rows), bf16),
        V((8, rows, e), bf16),
        V((2, 2, 2, quarter, e), bf16),
        V((2, 2, rows, e), bf16),
        V((2, rows, e), bf16),
        V((4 * rows, 4 * rows), bf16),
        V((2 * rows, 4 * rows), bf16),
        V((2 * rows, e), f32),
        V((2, 4, 2, 4, quarter, rows), bf16),
        V((2, 4, 2, 4, quarter, rows), bf16),
        V((7, 2, 4, quarter, rows), bf16),
        V((7, 2, 4, quarter, rows), bf16),
        V((2, 4, quarter, rows), bf16),
        V((2, 4, quarter, rows), bf16),
        V((7, quarter, rows), bf16),
        V((7, quarter, rows), bf16),
        V((2, e), f32),
        V((16, 2, e), f32),
        V((8, 2, e), f32),
        pltpu.SemaphoreType.DMA((copies,)),
        pltpu.SemaphoreType.DMA((copies,)),
        pltpu.SemaphoreType.DMA((9,)),
    ]
    shapes = (
        jax.ShapeDtypeStruct((rows, e), bf16),
        jax.ShapeDtypeStruct((rows, e), bf16),
        jax.ShapeDtypeStruct((half, rows), f32),
        jax.ShapeDtypeStruct((1, e), f32),
        jax.ShapeDtypeStruct((1, e), f32),
    )
    anywhere = pl.BlockSpec(memory_space=pl.ANY)
    results = pl.pallas_call(
        kernel,
        out_shape=shapes,
        in_specs=[anywhere] * 9,
        out_specs=(vmem,) * 5,
        scratch_shapes=scratch,
        compiler_params=pltpu.CompilerParams(
            collective_id=0, has_side_effects=True, vmem_limit_bytes=60 * 1024 * 1024
        ),
        cost_estimate=pl.CostEstimate(flops=16_000_000_000, bytes_accessed=5_000_000, transcendentals=2_100_000),
    )(
        q_hidden, d_hidden, positive.reshape(1, rows), query_part.reshape(1, rows), loss_weight.reshape(1, rows),
        doc_part.reshape(1, rows), norm_gain.reshape(1, e), norm_bias.reshape(1, e), proj,
    )
    dq, dd, d_proj, d_gain, d_bias = pl.pallas_call(
        hand_over,
        out_shape=shapes,
        in_specs=[vmem] * 5,
        out_specs=(vmem,) * 5,
        cost_estimate=pl.CostEstimate(flops=0, bytes_accessed=1_200_000, transcendentals=0),
    )(*results)
    return dq, dd, d_proj.T, d_gain.reshape(e), d_bias.reshape(e)


def solution(mesh):
    placed = (
        P(("pb", "dev"), None),
        P(("dev", "pb"), None),
        P(("pb", "dev")),
        P(("pb", "dev")),
        P(("dev", "pb")),
        P(("pb", "dev")),
        P(),
        P(),
        P(),
    )
    return jax.shard_map(
        per_device,
        mesh=mesh,
        in_specs=placed,
        out_specs=(P(("pb", "dev"), None), P(("dev", "pb"), None), P("pb", "dev"), P(), P()),
        check_vma=False,
    )
```

```python
import jax
import jax.numpy as jnp
from jax import lax
from jax.experimental import pallas as pl
from jax.experimental.pallas import tpu as pltpu
from jax.sharding import PartitionSpec as P

logit_scale = 100.0
f32, bf16 = jnp.float32, jnp.bfloat16
MESH = pl.DeviceIdType.MESH
rows, width = 128, 1024
half, quarter = rows // 2, rows // 4
copies = 200
OFFSETS = ((0, 0), (1, 0), (0, 1), (0, 3), (0, 2), (1, 2), (1, 1), (1, 3))
NT = (((1,), (1,)), ((), ()))


def kernel(
    qh_hbm, dh_hbm, pos_hbm, qpart_hbm, weight_hbm, dpart_hbm, gain_hbm, bias_hbm, proj_hbm,
    dq, dd, dproj, dgain, dbias,
    qh, dh, pos_in, qpart_in, weight_in, dpart_in, gain, bias,
    proj, qbuf, dbuf, dt, st, gt, unit, normed, recip, inv, out_t, lab_q, lab_d, labs, dlab, dcol, mst, sst, lsend, lbuf,
    lsef, lrel, gqp, cbuf, sbuf, qfold, qring, qx, gdp, dfold, dring, dx_buf,
    ge, gs, gns, hs0, hs1, r0, r1, h0, h1, f0, f1, gb, gba, gbb,
    send_sem, recv_sem, local_sem,
):
    pb, dev = lax.axis_index("pb"), lax.axis_index("dev")
    z, xl = pb // 2, lax.rem(pb, 2)
    y, xh, core = dev // 4, lax.rem(dev // 2, 2), lax.rem(dev, 2)

    def q_peer(dx, dy, dc=0):
        return (z * 2 + lax.rem(xl + dx, 2), lax.rem(y + dy, 4) * 4 + xh * 2 + lax.rem(core + dc, 2))

    def d_peer(dx, dz):
        return (lax.rem(z + dz, 4) * 2 + lax.rem(xl + dx, 2), y * 4 + lax.rem(xh + dx, 2) * 2 + core)

    started = []

    def send(src, dst, peer):
        n = len(started)
        copy = pltpu.make_async_remote_copy(
            src_ref=src, dst_ref=dst, send_sem=send_sem.at[n], recv_sem=recv_sem.at[n],
            device_id=peer, device_id_type=MESH,
        )
        copy.start()
        started.append(copy)
        return copy

    def arrive(*copies):
        for copy in copies:
            copy.wait_recv()

    q_offsets = [(dx, dy, dc) for dx in range(2) for dy in range(4) for dc in range(2)]
    d_offsets = [(dx, dz) for dx in range(2) for dz in range(4)]

    loads = []
    for n, (src, dst) in enumerate((
        (qh_hbm, qh), (dh_hbm, dh), (proj_hbm, proj), (gain_hbm, gain), (bias_hbm, bias),
        (pos_hbm, pos_in), (qpart_hbm, qpart_in), (weight_hbm, weight_in), (dpart_hbm, dpart_in),
    )):
        loads.append(pltpu.make_async_copy(src, dst, local_sem.at[n]))
        loads[-1].start()
    barrier = pltpu.get_barrier_semaphore()
    peers = [q_peer(*o) for o in q_offsets[1:]] + [d_peer(*o) for o in d_offsets[1:]]
    for peer in peers:
        pl.semaphore_signal(barrier, inc=1, device_id=peer, device_id_type=MESH)

    for n in (0, 1, 3, 4, 5, 6, 7, 8):
        loads[n].wait()
    lab_q[...] = jnp.zeros((8, rows), f32)
    lab_q[0:1, :] = pos_in[...].astype(f32)
    lab_q[1:2, :] = qpart_in[...].astype(f32)
    lab_q[2:3, :] = weight_in[...].astype(f32)
    lab_d[...] = jnp.broadcast_to(dpart_in[...].astype(f32), (8, rows))
    values = jnp.concatenate([qh[...], dh[...]], axis=0).astype(f32)
    centred = values - jnp.mean(values, axis=1, keepdims=True)
    r = lax.rsqrt(jnp.mean(centred * centred, axis=1, keepdims=True) + 1e-05)
    norm = centred * r
    recip[...] = r
    normed[...] = norm
    normal_out = (norm * gain[...] + bias[...]).astype(bf16)
    loads[2].wait()
    pl.semaphore_wait(barrier, len(peers))

    block = 8 * rows

    def q_at(core_index, k, offset=0):
        return pl.multiple_of(core_index * block + k * rows + offset, quarter)

    embed = jnp.dot(normal_out, proj[...], preferred_element_type=f32)
    i = lax.rsqrt(jnp.sum(embed * embed, axis=1, keepdims=True) + 1e-06)
    inv[...] = i
    u = embed * i
    unit[...] = u
    qbuf[pl.ds(q_at(core, 0), rows), :] = u[:rows].astype(bf16)
    dbuf[0:rows, :] = u[rows:].astype(bf16)

    def q_part(k, first, count):
        return qbuf.at[pl.ds(q_at(core, k, first * quarter), count * quarter), :]

    def d_part(k, first, count):
        return dbuf.at[pl.ds(k * rows + first * quarter, count * quarter), :]

    def to_sibling(k):
        part = qbuf.at[pl.ds(pl.multiple_of(core * block + k * rows, rows), rows), :]
        return send(part, part, q_peer(0, 0, 1))

    q_got, d_got, sib = {}, {}, {}

    def hop(part, got, peer, k, span, to, way):
        got[to, span] = send(part(k, *span), part(to, *span), peer(1, 0) if way == 0 else peer(0, way))

    towers = ((q_part, q_got, q_peer), (d_part, d_got, d_peer))
    A, B, A0, A1, B0, B1 = (0, 2), (2, 2), (0, 1), (1, 1), (2, 1), (3, 1)
    for spans in (((A, 3, 1), (B, 2, 3), (A0, 1, 0), (B0, 1, 0)), ((B, 3, 1), (A, 2, 3), (A1, 1, 0), (B1, 1, 0))):
        for tower in towers:
            for span, to, way in spans:
                hop(*tower, 0, span, to, way)
    sib[0] = to_sibling(0)
    lab_copies = []
    for dx, dy, dc in q_offsets[1:]:
        k = OFFSETS.index((dx, (4 - dy) % 4))
        dst = labs.at[:, pl.ds(pl.multiple_of(core * block + k * rows, rows), rows)]
        lab_copies.append(send(lab_q, dst, q_peer(dx, dy, dc)))
    for dx, dz in d_offsets[1:]:
        lab_copies.append(send(lab_d, dlab.at[OFFSETS.index((dx, (4 - dz) % 4))], d_peer(dx, dz)))
    labs[:, pl.ds(pl.multiple_of(core * block, rows), rows)] = lab_q[...]
    dlab[0] = lab_d[...]
    out_t[:, 0 : 2 * rows] = normal_out.T
    out_sib = send(out_t.at[:, pl.ds(0, 2 * rows)], out_t.at[:, pl.ds(2 * rows, 2 * rows)], q_peer(0, 0, 1))
    for tower in towers:
        arrive(tower[1][1, A0])
        hop(*tower, 1, A0, 7, 1)
    for tower in towers:
        arrive(tower[1][3, A])
        hop(*tower, 3, A, 4, 1)
        arrive(tower[1][2, B])
        hop(*tower, 2, B, 4, 3)
    for tower in towers:
        arrive(tower[1][1, B0])
        hop(*tower, 1, B0, 6, 3)
        arrive(tower[1][1, A1])
        hop(*tower, 1, A1, 7, 1)
        arrive(tower[1][1, B1])
        hop(*tower, 1, B1, 6, 3)
    for tower in towers:
        arrive(tower[1][3, B])
        hop(*tower, 3, B, 7, 0)
        arrive(tower[1][2, A])
        hop(*tower, 2, A, 6, 0)
    sib[1] = to_sibling(1)
    sib[2], sib[3] = to_sibling(2), to_sibling(3)
    arrive(*lab_copies)

    for k in range(8):
        dcol[k * rows : (k + 1) * rows, :] = jnp.broadcast_to(dlab[k, 0:1, :], (rows, rows)).T

    def transpose_docs(first, count):
        for k in range(first, first + count):
            dt[:, k * rows : (k + 1) * rows] = dbuf[k * rows : (k + 1) * rows, :].T

    def lane(wide):
        return lax.broadcasted_iota(jnp.int32, (rows, wide), 0).astype(f32)

    def bases(k):
        to_pb, to_dev = d_peer(*OFFSETS[k])
        return ((to_dev * 8 + to_pb) * rows).astype(f32)

    def pair_cols(core_index, m, count=1):
        return pl.ds(pl.multiple_of(core_index * block + m * 2 * rows, 2 * rows), count * 2 * rows)

    def score(first, count, piece, cols):
        wide = cols.size
        s = logit_scale * lax.dot_general(
            dbuf[first * rows : (first + count) * rows, :], qbuf[cols, :], NT, preferred_element_type=f32
        )
        pos, part = labs[0:1, cols], labs[1:2, cols]
        masked = []
        for n in range(count):
            k = first + n
            col = jnp.concatenate([dcol[k * rows : (k + 1) * rows, :]] * (wide // rows), axis=1)
            valid = jnp.logical_or(part != col, lane(wide) == pos - bases(k))
            masked.append(jnp.where(valid, s[n * rows : (n + 1) * rows], jnp.float32(-1e30)))
        top = jnp.full((1, wide), -1e4, f32)
        for m in masked:
            top = jnp.maximum(top, jnp.max(m, axis=0, keepdims=True))
        total = jnp.zeros((1, wide), f32)
        for n, m in enumerate(masked):
            p = jnp.exp(m - top)
            total = total + jnp.sum(p, axis=0, keepdims=True)
            st[(first + n) * rows : (first + n + 1) * rows, cols] = p
        mst[piece, :, cols] = top
        sst[piece, :, cols] = total

    pieces = ((0, 4), (4, 2), (6, 2))

    def scores(piece, m, count):
        def body(c, carry):
            score(*pieces[piece], piece, pair_cols(c, m, count))
            return carry

        lax.fori_loop(0, 2, body, 0)

    transpose_docs(0, 4)
    arrive(sib[0], sib[1], sib[2], sib[3])
    scores(0, 0, 1)
    scores(0, 1, 1)

    for a, b in ((A0, B0), (A1, B1)):
        for tower in towers:
            arrive(tower[1][7, a])
            hop(*tower, 7, a, 5, 1)
            arrive(tower[1][6, b])
            hop(*tower, 6, b, 5, 3)
    arrive(q_got[4, A], q_got[4, B])
    sib[4] = to_sibling(4)
    arrive(q_got[7, B], q_got[6, A])
    sib[6], sib[7] = to_sibling(6), to_sibling(7)
    arrive(d_got[7, B], d_got[6, A], d_got[4, A], d_got[4, B])
    transpose_docs(6, 2)
    transpose_docs(4, 1)
    scores(2, 0, 2)
    arrive(sib[6], sib[7])
    scores(0, 3, 1)
    scores(2, 3, 1)

    arrive(*(q_got[5, span] for span in (A0, B0, A1, B1)))
    sib[5] = to_sibling(5)
    arrive(*(d_got[5, span] for span in (A0, B0, A1, B1)))
    transpose_docs(5, 1)
    scores(1, 0, 2)
    arrive(sib[4], sib[5])
    scores(1, 2, 2)
    scores(0, 2, 1)
    scores(2, 2, 1)

    top = jnp.maximum(jnp.maximum(mst[0], mst[1]), mst[2])
    total = sum(sst[b] * jnp.exp(mst[b] - top) for b in range(3))
    local = top + jnp.log(jnp.maximum(total, 1e-37))
    places = []
    for n in range(16):
        c, (dx, dy) = n // 8, OFFSETS[n % 8]
        places.append(c * 8 + lax.rem(y + dy, 4) * 2 + lax.rem(xl + dx, 2))
        lsend[pl.ds(places[-1], 1), :] = local[:, n * rows : (n + 1) * rows]
    lse_copies = [send(lsend, lbuf.at[s], q_peer(*q_offsets[s])) for s in range(1, 16)]
    lbuf[0] = lsend[...]
    arrive(*lse_copies)
    every = lbuf[...]
    top = jnp.max(every, axis=0)
    lsef[...] = top + jnp.log(jnp.sum(jnp.exp(every - top[None]), axis=0))
    for n, place in enumerate(places):
        lrel[:, n * rows : (n + 1) * rows] = lsef[pl.ds(place, 1), :]
    for b in range(3):
        sst[b] = jnp.exp(mst[b] - lrel[...])

    def grads(c, m, ks):
        cols = pair_cols(c, m)
        pos, weight = labs[0:1, cols], labs[2:3, cols]
        for k in ks:
            scale = sst[0 if k < 4 else 1 if k < 6 else 2, :, cols]
            hit = jnp.where(lane(2 * rows) == pos - bases(k), jnp.float32(1), jnp.float32(0))
            prob = st[k * rows : (k + 1) * rows, cols] * scale
            gt[k * rows : (k + 1) * rows, cols] = (weight * (prob - hit)).astype(bf16)

    def grads_of(ms, ks):
        def body(c, carry):
            for m in ms:
                grads(c, m, ks)
            return carry

        lax.fori_loop(0, 2, body, 0)


    def doc_terms(m):
        def body(j, carry):
            cols = pl.ds(pl.multiple_of(j * 512, 512), 512)
            v = jnp.dot(
                gt[2 * m * rows : 2 * (m + 1) * rows, :], qbuf[:, cols], preferred_element_type=f32
            ).astype(bf16)
            gdp[2 * m, :, cols] = v[:rows]
            gdp[2 * m + 1, :, cols] = v[rows:]
            return carry

        lax.fori_loop(0, 2, body, 0)

    cores = {}

    def query_terms(m, other):
        cols = pair_cols(1 - core if other else core, m)

        v = jnp.dot(dt[...], gt[:, cols], preferred_element_type=f32).astype(bf16)
        gqp[other, 2 * m] = v[:, :rows]
        gqp[other, 2 * m + 1] = v[:, rows:]
        if other:
            span = pl.ds(2 * m, 2)
            cores[m] = send(gqp.at[1, span], cbuf.at[span], q_peer(0, 0, 1))

    def both_cores(k):
        if k // 2 in cores:
            arrive(cores.pop(k // 2))
        sbuf[k] = (gqp[0, k].astype(f32) + cbuf[k].astype(f32)).astype(bf16)

    slots = ((0, 2, 3, 4), (1, 6, 7, 5))

    def part_of(h, c, size):
        return pl.ds((2 * c + h) * size, size)

    def far_terms(src, fold, ring, peer, size, dx):
        far = slots[dx][3]
        return [
            [send(src.at[far, part_of(h, c, size), :], fold.at[dx, h, c], peer(0, 3 if h else 1)) for h in range(2)]
            for c in range(2)
        ]

    def near_terms(src, fold, ring, peer, size, dx):
        got = []
        for c in range(2):
            for h, way in ((1, 1), (0, 3)):
                part = part_of(h, c, size)
                got.append(send(src.at[slots[dx][1 if h else 2], part, :], ring.at[dx, 1 - h, part, :], peer(0, way)))
        return got

    def merged(src, fold, ring, peer, size, dx, c, waits):
        got = []
        for h in range(2):
            k, part = slots[dx][1 + h], part_of(h, c, size)
            rows_of = slice((2 * c + h) * size, (2 * c + h + 1) * size)
            arrive(waits[c][h])
            src[k, rows_of, :] = (src[k, rows_of, :].astype(f32) + fold[dx, h, c].astype(f32)).astype(bf16)
            got.append(send(src.at[k, part, :], ring.at[dx, h, part, :], peer(0, 3 if h else 1)))
        return got

    def ring_sum(src, ring, dx, low, size):
        span = slice(low, low + size)
        return src[dx, span, :].astype(f32) + ring[dx, 0, span, :].astype(f32) + ring[dx, 1, span, :].astype(f32)

    def across(src, ring, buf, peer, size, c):
        span = pl.ds(c * 2 * size, 2 * size)
        buf[0, c * 2 * size : (c + 1) * 2 * size, :] = ring_sum(src, ring, 1, c * 2 * size, 2 * size).astype(bf16)
        return send(buf.at[0, span, :], buf.at[1, span, :], peer(1, 0))

    D = (gdp, dfold, dring, d_peer, quarter)
    Q = (sbuf, qfold, qring, q_peer, width // 4)
    grads(1 - core, 2, range(8))
    query_terms(2, 1)
    grads(core, 2, range(8))
    query_terms(2, 0)
    grads_of((0, 1, 3), (4, 5))
    doc_terms(2)
    d_fold1 = far_terms(*D, 1)
    both_cores(5)
    q_fold1 = far_terms(*Q, 1)
    grads_of((3,), (0, 1, 2, 3, 6, 7))
    query_terms(3, 1)
    grads_of((0, 1), (6, 7))
    doc_terms(3)
    d_near1 = near_terms(*D, 1)
    query_terms(3, 0)
    both_cores(6)
    both_cores(7)
    q_near1 = near_terms(*Q, 1)
    both_cores(4)
    grads_of((0, 1), (0, 1, 2, 3))
    query_terms(1, 1)
    d_ring1 = [merged(*D, 1, 0, d_fold1)]
    q_ring1 = [merged(*Q, 1, 0, q_fold1)]
    d_ring1.append(merged(*D, 1, 1, d_fold1))
    q_ring1.append(merged(*Q, 1, 1, q_fold1))
    d_fold0 = far_terms(*D, 0)
    q_fold0 = far_terms(*Q, 0)
    query_terms(0, 1)
    doc_terms(1)
    d_near0 = near_terms(*D, 0)
    query_terms(1, 0)
    both_cores(2)
    both_cores(3)
    q_near0 = near_terms(*Q, 0)
    doc_terms(0)
    query_terms(0, 0)
    both_cores(1)
    both_cores(0)
    d_across, q_across = [], []
    arrive(*d_near1, *q_near1)
    for c in range(2):
        arrive(*d_ring1[c])
        d_across.append(across(gdp, dring, dx_buf, d_peer, quarter, c))
        arrive(*q_ring1[c])
        q_across.append(across(sbuf, qring, qx, q_peer, width // 4, c))
    d_ring0, q_ring0 = [], []
    for c in range(2):
        d_ring0 += merged(*D, 0, c, d_fold0)
        q_ring0 += merged(*Q, 0, c, q_fold0)

    left = lax.broadcasted_iota(jnp.int32, (rows, rows), 1) < half
    ge_copies = []

    def embed_rows(total, low):
        span = slice(low, low + rows)
        g_unit, uu = logit_scale * total, unit[span, :]
        g = (g_unit - uu * jnp.sum(uu * g_unit, axis=1, keepdims=True)) * inv[span, :]
        for j in range(4):
            b0, b1 = g[:, 2 * j * rows : (2 * j + 1) * rows], g[:, (2 * j + 1) * rows : (2 * j + 2) * rows]
            n0 = jnp.where(left, b0, pltpu.roll(b1, half, 1))
            n1 = jnp.where(left, pltpu.roll(b0, half, 1), b1)
            ge[span, j * rows : (j + 1) * rows] = jnp.where(core == 0, n0, n1).astype(bf16)
            gs[span, j * rows : (j + 1) * rows] = jnp.where(core == 0, n1, n0).astype(bf16)
        ge_copies.append(send(gs.at[pl.ds(low, rows), :], ge.at[pl.ds(2 * rows + low, rows), :], q_peer(0, 0, 1)))
        return g.astype(bf16)

    arrive(*d_near0, *d_ring0, *d_across)
    g_doc = embed_rows(ring_sum(gdp, dring, 0, 0, rows) + dx_buf[1].astype(f32), rows)
    arrive(*q_near0, *q_ring0, *q_across)
    g_query = embed_rows((ring_sum(sbuf, qring, 0, 0, width) + qx[1].astype(f32)).T, 0)
    g = jnp.concatenate([g_query, g_doc], axis=0)
    gn = lax.dot_general(g, proj[...], NT, preferred_element_type=f32)
    nn = normed[...]
    gns[...] = gn
    gb[0:1, :] = jnp.sum(gn * nn, axis=0, keepdims=True)
    gb[1:2, :] = jnp.sum(gn, axis=0, keepdims=True)
    order = (y * 2 + xl) * 2 + core
    gb_copies = [send(gb, gba.at[order], q_peer(*o)) for o in q_offsets[1:]]
    gba[order] = gb[...]

    low_left = left[:half]
    arrive(out_sib, *ge_copies)

    def head(n, carry):
        for a in range(2):
            v = jnp.dot(
                out_t[pl.ds(pl.multiple_of((2 * n + a) * rows, rows), rows), :], ge[...], preferred_element_type=f32
            )
            for j in range(4):
                upper, lower = v[:half, j * rows : (j + 1) * rows], v[half:, j * rows : (j + 1) * rows]
                for b in range(2):
                    if b == 0:
                        w = jnp.where(low_left, upper, pltpu.roll(lower, half, 1)).astype(bf16)
                    else:
                        w = jnp.where(low_left, pltpu.roll(upper, half, 1), lower).astype(bf16)
                    hs0[b, n, a, j] = w[:quarter]
                    hs1[(a + b) % 2, j, b, n] = w[quarter:]
        return carry

    lax.fori_loop(0, 4, head, 0)
    diagonal = lax.rem(xl + xh, 2)
    first0, first1 = [], []
    for s, (dx, dz) in enumerate(d_offsets[1:]):
        first0.append(send(hs0.at[lax.rem(xh + dx, 2), lax.rem(z + dz, 4)], r0.at[s], d_peer(dx, dz)))
        dy = dz
        first1.append(send(hs1.at[lax.rem(diagonal + dx, 2), lax.rem(y + dy, 4)], r1.at[s], q_peer(dx, dy)))
    gn, nn = gns[...], normed[...]
    scaled = gn * gain[...]
    grad_h = recip[...] * (
        scaled - jnp.mean(scaled, axis=1, keepdims=True) - nn * jnp.mean(scaled * nn, axis=1, keepdims=True)
    )
    dq[...] = grad_h[:rows].astype(bf16)
    dd[...] = grad_h[rows:].astype(bf16)

    arrive(*gb_copies)
    acc = gba[0]
    for n in range(1, 16):
        acc = acc + gba[n]
    order = z * 2 + xh
    gbb[order] = acc
    gb_copies = [send(gbb.at[order], gbb.at[order], d_peer(*o)) for o in d_offsets[1:]]

    def total_of(own, got):
        return own.astype(f32) + sum(got[n].astype(f32) for n in range(7))

    arrive(*first0)
    h0[...] = total_of(hs0[xh, z], r0).astype(bf16)
    second0 = [
        send(h0.at[lax.rem(xl + dx, 2), lax.rem(y + dy, 4)], f0.at[s], q_peer(dx, dy))
        for s, (dx, dy) in enumerate(d_offsets[1:])
    ]
    arrive(*first1)
    h1[...] = total_of(hs1[diagonal, y], r1).astype(bf16)
    second1 = [
        send(h1.at[lax.rem(xh + dx, 2), lax.rem(z + dz, 4)], f1.at[s], d_peer(dx, dz))
        for s, (dx, dz) in enumerate(d_offsets[1:])
    ]
    arrive(*second0, *second1)
    final = jnp.concatenate([total_of(h0[xl, y], f0), total_of(h1[xh, z], f1)], axis=0)
    dproj[:, 0:half] = final[:, :half].T
    dproj[:, half:rows] = final[:, half:].T

    arrive(*gb_copies)
    acc = gbb[0]
    for n in range(1, 8):
        acc = acc + gbb[n]
    dgain[...] = acc[0:1]
    dbias[...] = acc[1:2]

    for copy in started:
        copy.wait_send()


def hand_over(*refs):
    for src, dst in zip(refs[:5], refs[5:]):
        dst[...] = src[...]


def per_device(
    q_hidden, d_hidden, positive, query_part, doc_part, loss_weight, norm_gain, norm_bias, proj
):
    vmem = pl.BlockSpec(memory_space=pltpu.VMEM)
    V = pltpu.VMEM
    e = width
    scratch = [
        V((rows, e), bf16),
        V((rows, e), bf16),
        V((1, rows), jnp.int32),
        V((1, rows), jnp.int32),
        V((1, rows), bf16),
        V((1, rows), jnp.int32),
        V((1, e), f32),
        V((1, e), f32),
        V((e, e), bf16),
        V((16 * rows, e), bf16),
        V((8 * rows, e), bf16),
        V((e, 8 * rows), bf16),
        V((8 * rows, 16 * rows), f32),
        V((8 * rows, 16 * rows), bf16),
        V((2 * rows, e), f32),
        V((2 * rows, e), f32),
        V((2 * rows, 1), f32),
        V((2 * rows, 1), f32),
        V((e, 4 * rows), bf16),
        V((8, rows), f32),
        V((8, rows), f32),
        V((8, 16 * rows), f32),
        V((8, 8, rows), f32),
        V((8 * rows, rows), f32),
        V((3, 1, 16 * rows), f32),
        V((3, 1, 16 * rows), f32),
        V((16, rows), f32),
        V((16, 16, rows), f32),
        V((16, rows), f32),
        V((1, 16 * rows), f32),
        V((2, 8, e, rows), bf16),
        V((8, e, rows), bf16),
        V((8, e, rows), bf16),
        V((2, 2, 2, e // 4, rows), bf16),
        V((2, 2, e, rows), bf16),
        V((2, e, rows), bf16),
        V((8, rows, e), bf16),
        V((2, 2, 2, quarter, e), bf16),
        V((2, 2, rows, e), bf16),
        V((2, rows, e), bf16),
        V((4 * rows, 4 * rows), bf16),
        V((2 * rows, 4 * rows), bf16),
        V((2 * rows, e), f32),
        V((2, 4, 2, 4, quarter, rows), bf16),
        V((2, 4, 2, 4, quarter, rows), bf16),
        V((7, 2, 4, quarter, rows), bf16),
        V((7, 2, 4, quarter, rows), bf16),
        V((2, 4, quarter, rows), bf16),
        V((2, 4, quarter, rows), bf16),
        V((7, quarter, rows), bf16),
        V((7, quarter, rows), bf16),
        V((2, e), f32),
        V((16, 2, e), f32),
        V((8, 2, e), f32),
        pltpu.SemaphoreType.DMA((copies,)),
        pltpu.SemaphoreType.DMA((copies,)),
        pltpu.SemaphoreType.DMA((9,)),
    ]
    shapes = (
        jax.ShapeDtypeStruct((rows, e), bf16),
        jax.ShapeDtypeStruct((rows, e), bf16),
        jax.ShapeDtypeStruct((half, rows), f32),
        jax.ShapeDtypeStruct((1, e), f32),
        jax.ShapeDtypeStruct((1, e), f32),
    )
    anywhere = pl.BlockSpec(memory_space=pl.ANY)
    results = pl.pallas_call(
        kernel,
        out_shape=shapes,
        in_specs=[anywhere] * 9,
        out_specs=(vmem,) * 5,
        scratch_shapes=scratch,
        compiler_params=pltpu.CompilerParams(
            collective_id=0, has_side_effects=True, vmem_limit_bytes=60 * 1024 * 1024
        ),
        cost_estimate=pl.CostEstimate(flops=16_000_000_000, bytes_accessed=5_000_000, transcendentals=2_100_000),
    )(
        q_hidden, d_hidden, positive.reshape(1, rows), query_part.reshape(1, rows), loss_weight.reshape(1, rows),
        doc_part.reshape(1, rows), norm_gain.reshape(1, e), norm_bias.reshape(1, e), proj,
    )
    dq, dd, d_proj, d_gain, d_bias = pl.pallas_call(
        hand_over,
        out_shape=shapes,
        in_specs=[vmem] * 5,
        out_specs=(vmem,) * 5,
        cost_estimate=pl.CostEstimate(flops=0, bytes_accessed=1_200_000, transcendentals=0),
    )(*results)
    return dq, dd, d_proj.T, d_gain.reshape(e), d_bias.reshape(e)


def solution(mesh):
    placed = (
        P(("pb", "dev"), None),
        P(("dev", "pb"), None),
        P(("pb", "dev")),
        P(("pb", "dev")),
        P(("dev", "pb")),
        P(("pb", "dev")),
        P(),
        P(),
        P(),
    )
    return jax.shard_map(
        per_device,
        mesh=mesh,
        in_specs=placed,
        out_specs=(P(("pb", "dev"), None), P(("dev", "pb"), None), P("pb", "dev"), P(), P()),
        check_vma=False,
    )
```
